128 devices in a mesh: pix: 32 (over x, z, core), tp: 4 (over y).
Axes of the slice: x: 4, y: 4, z: 4, core: 2. Of those that a mesh axis runs over, the one named last changes fastest.
Arguments:
- latent: bfloat16 [131072, 512], P(('pix', 'tp')), may hold values from -6 to 6
- norm_gain: float32 [512], replicated, may hold values from 0.5 to 2
- w_in: bfloat16 [512, 2048], P(None, 'tp'), may hold values from -0.25 to 0.25
- w_out: bfloat16 [2048, 512], P('tp'), may hold values from -0.125 to 0.125
- send_rows: int32 [16384, 32], P(('pix', 'tp')), may hold values from 0 to 1023
- obs_src: int32 [524288], P(('pix', 'tp')), may hold values from 0 to 5119
- obs_feat: bfloat16 [524288, 128], P(('pix', 'tp')), may hold values from -6 to 6
- obs_inst: int32 [524288], P(('pix', 'tp')), may hold values from 0 to 31
- inst_embed: float32 [32, 2048], replicated, may hold values from -3 to 3
- w_dec: bfloat16 [512, 2048], replicated, may hold values from -0.25 to 0.25
- w_feat: bfloat16 [128, 2048], replicated, may hold values from -0.5 to 0.5
- w_head: bfloat16 [2048, 128], replicated, may hold values from -0.125 to 0.125
Outputs:
- latent_out: bfloat16 [131072, 512], P(('pix', 'tp'))
- decoded: float32 [524288, 128], P(('pix', 'tp'))
The draws below stay inside these ranges and needn't reach their ends.
All inputs are finite; a program needn't handle non-finite values.
Results may differ from the reference program's by a relative error of at most 0.005.
Values may be sent and summed in bfloat16 or wider, within the bound.
A program may use at most 64 MiB of HBM per device.

```python
import math
import jax
import jax.numpy as jnp
import numpy as np
from jax import lax

D = 512
FF = 2048
CH = 128
FEAT = 128
INSTR = 32
ROWS_DEV = 1024
OBS_DEV = 4096
CAP = 32
CELLS = 131072
OBS = 524288
LISTS = 16384
N_PIX = 32
N_TP = 4


def place_ends(drawn, stream_key, least, top_value):
    extent = drawn.shape
    spot = [jax.random.randint(jax.random.fold_in(stream_key, axis), (), 0, extent[axis]) for axis in range(len(extent))]
    drawn = drawn.at[tuple(spot)].set(least)
    longest = extent.index(max(extent))
    spot[longest] = (spot[longest] + 1) % extent[longest]
    return drawn.at[tuple(spot)].set(top_value)


def levels(stream_key, extent, shards, smallest, high):
    def one(position, shards_of):
        heights = jax.random.uniform(jax.random.fold_in(jax.random.fold_in(stream_key, 6), position), (shards_of,), jnp.float32, smallest / len(shards), high / len(shards))
        return jnp.repeat(jnp.exp(heights), extent[position] // shards_of).reshape((-1,) + (1,) * (len(extent) - position - 1))

    factor_of = one(*shards[0])
    for cut in shards[1:]:
        factor_of = factor_of * one(*cut)
    return factor_of


def rank_bounds(amount, slope):
    weights = [(1 << 20) // math.isqrt(standing ** slope) + 1 for standing in range(1, amount + 1)]
    width = 1 + sum(weights) // (1 << 30)
    return np.cumsum(np.array([max(1, weight // width) for weight in weights]))


def ranked_ids(rng, extent, amount, slope):
    grid = rank_bounds(amount, slope)
    ticket = jax.random.randint(jax.random.fold_in(rng, 1), extent, 0, int(grid[amount - 1]))
    grade = jnp.searchsorted(jnp.asarray(grid, jnp.int32), ticket, side="right")
    return jax.random.permutation(jax.random.fold_in(rng, 2), amount)[grade].astype(jnp.int32)


def bell_draw(stream_key, extent, scale, reach, pieces=(), kind=jnp.bfloat16):
    factor_of = levels(stream_key, extent, pieces, -0.22, 0.18) if pieces else 1.0
    entries = jax.random.normal(stream_key, extent, jnp.float32) * scale * factor_of
    return jnp.minimum(jnp.maximum(entries, -reach), reach).astype(kind)


def setup_inputs(seed: int = 0) -> dict:
    arg_keys = jax.random.split(jax.random.key(seed), 13)
    return {
        "latent": bell_draw(arg_keys[0], (CELLS, D), 1.0, 6.0, ((0, 128),)),
        "norm_gain": jnp.clip(jnp.exp(jax.random.uniform(arg_keys[1], (D,), jnp.float32, math.log(0.5), math.log(2.0))), 0.5, 2.0),
        "w_in": bell_draw(arg_keys[2], (D, FF), D ** -0.5, 0.25, ((1, 4),)),
        "w_out": bell_draw(arg_keys[3], (FF, D), FF ** -0.5, 0.125, ((0, 4),)),
        "send_rows": place_ends(jax.random.randint(arg_keys[4], (LISTS, CAP), 0, ROWS_DEV), jax.random.fold_in(arg_keys[4], 1), 0, ROWS_DEV - 1).astype(jnp.int32),
        "obs_src": place_ends(jax.random.randint(arg_keys[5], (OBS,), 0, ROWS_DEV + N_PIX * N_TP * CAP), jax.random.fold_in(arg_keys[5], 1), 0, (ROWS_DEV + N_PIX * N_TP * CAP) - 1).astype(jnp.int32),
        "obs_feat": bell_draw(arg_keys[6], (OBS, FEAT), 1.0, 6.0, ((0, 128),)),
        "obs_inst": place_ends(ranked_ids(arg_keys[7], (OBS,), INSTR, 2), jax.random.fold_in(arg_keys[7], 3), 0, INSTR - 1).astype(jnp.int32),
        "inst_embed": bell_draw(arg_keys[8], (INSTR, FF), 0.5, 3.0, (), jnp.float32),
        "w_dec": bell_draw(arg_keys[9], (D, FF), D ** -0.5, 0.25),
        "w_feat": bell_draw(arg_keys[10], (FEAT, FF), FEAT ** -0.5, 0.5),
        "w_head": bell_draw(arg_keys[11], (FF, CH), FF ** -0.5, 0.125),
    }


def layer_norm(block, norm_gain):
    values = block.astype(jnp.float32)
    center = values - lax.optimization_barrier(jnp.mean(values, axis=-1, keepdims=True))
    spread = lax.optimization_barrier(jnp.mean(center * center, axis=-1, keepdims=True))
    return (center * lax.rsqrt(spread + 1e-05) * norm_gain).astype(jnp.bfloat16)

def reference(latent, norm_gain, w_in, w_out, send_rows, obs_src, obs_feat, obs_inst, inst_embed, w_dec, w_feat, w_head):
    devices = N_PIX * N_TP

    def process(block):
        normed = layer_norm(block, norm_gain)
        inner = jax.nn.gelu(jnp.dot(normed, w_in, preferred_element_type=jnp.float32)).astype(jnp.bfloat16)
        update = jnp.dot(inner, w_out, preferred_element_type=jnp.float32)
        return (block.astype(jnp.float32) + update).astype(jnp.bfloat16)
    latent_out = lax.map(process, latent.reshape(devices, ROWS_DEV, D)).reshape(CELLS, D)
    owner = jnp.arange(OBS_DEV * devices, dtype=jnp.int32) // OBS_DEV
    remote = obs_src - ROWS_DEV
    clipped = jnp.maximum(remote, 0)
    source = clipped // CAP
    slot = clipped % CAP
    flat_lists = send_rows.reshape(-1)
    listed = flat_lists[((source * devices + owner) * CAP + slot).astype(jnp.int32)]
    cell = jnp.where(remote < 0, owner * ROWS_DEV + obs_src, source * ROWS_DEV + listed).astype(jnp.int32)

    def decode(items):
        cells, feats, insts = items
        gathered = latent_out[cells]
        pre = jnp.dot(gathered, w_dec, preferred_element_type=jnp.float32)
        pre = pre + jnp.dot(feats, w_feat, preferred_element_type=jnp.float32)
        pre = pre + inst_embed[insts]
        hidden = jax.nn.gelu(pre).astype(jnp.bfloat16)
        return jnp.dot(hidden, w_head, preferred_element_type=jnp.float32)
    decoded = lax.map(decode, (cell.reshape(devices, OBS_DEV), obs_feat.reshape(devices, OBS_DEV, FEAT), obs_inst.reshape(devices, OBS_DEV)))
    return (latent_out, decoded.reshape(OBS_DEV * devices, CH))
```

```python
import functools

import jax
import jax.numpy as jnp
from jax import lax
from jax.experimental import pallas as pl
from jax.experimental.pallas import tpu as pltpu
from jax.sharding import PartitionSpec as P

MESH = pl.DeviceIdType.MESH
F32, BF16 = jnp.float32, jnp.bfloat16

ROWS = 1024
D = 512
FF = 2048
CAP = 32
NDEV = 128
PER = 8
CHUNKS = NDEV // PER
CROWS = PER * CAP
RAW = 8
MUL, INV = 37, 45
BLOCK = 512
OBS = 4096


def gelu(x):
    u = x * (0.7978845608028654 + 0.035677408136300125 * (x * x))
    h = 0.5 * x
    return h + h * jnp.tanh(u)


def coords():
    p, y = lax.axis_index("pix"), lax.axis_index("tp")
    return p // 8, (p // 2) % 4, p % 2, y


def partner(k):
    x, z, c, y = coords()
    kk = (MUL * k) % NDEV
    dy, dc, dz, dx = kk % 4, (kk // 4) % 2, (kk // 8) % 4, kk // 32
    return ((x + dx) % 4) * 8 + ((z + dz) % 4) * 2 + (c + dc) % 2, (y + dy) % 4


def process(rows, gain, w_ref):
    values = rows.astype(F32)
    center = values - jnp.mean(values, axis=-1, keepdims=True)
    spread = jnp.mean(center * center, axis=-1, keepdims=True)
    normed = (center * lax.rsqrt(spread + 1e-05) * gain).astype(BF16)
    acc = values
    for d in range(4):
        inner = gelu(jnp.dot(normed, w_ref[d, 0].reshape(D, D), preferred_element_type=F32)).astype(BF16)
        acc = acc + jnp.dot(inner, w_ref[d, 1].reshape(D, D), preferred_element_type=F32)
    return acc.astype(BF16)


def exchange_kernel(
    latent, gain, w_in, w_out, send_rows, obs_src, table, index,
    w, send, raw, upd, ids, load_sem, w_send, w_recv, send_sem, recv_sem, out_sem, s2, s3, s4,
):
    x, z, c, y = coords()
    pix = lax.axis_index("pix")
    sib = pix + 1 - 2 * c
    xs = [(((x + d) % 4) * 8 + z * 2 + c, y) for d in (1, 2, 3)]
    zs = [(x * 8 + ((z + d) % 4) * 2 + c, y) for d in (1, 2, 3)]
    ys = [(pix, (y + 4 - d) % 4) for d in (1, 2, 3)]

    def signal(sem, who):
        for dev in who:
            pl.semaphore_signal(sem, inc=1, device_id=dev, device_id_type=MESH)

    barrier = pltpu.get_barrier_semaphore()
    signal(barrier, ys + zs + xs + [(sib, y)])
    loads = [
        pltpu.make_async_copy(w_in, w.at[0, 0], load_sem.at[0]),
        pltpu.make_async_copy(w_out, w.at[0, 1], load_sem.at[1]),
    ]
    for load in loads:
        load.start()

    ids[...] = jnp.concatenate(
        [send_rows[...].astype(F32), jnp.zeros((NDEV, NDEV - CAP), F32)], axis=1
    ).T[:CAP]

    r = obs_src[...]
    s = jnp.maximum(r - ROWS, 0) // CAP
    sp, st = s // 4, s % 4
    kk = (
        (y - st + 4) % 4
        + 4 * ((c - sp % 2 + 2) % 2)
        + 8 * ((z - (sp // 2) % 4 + 4) % 4)
        + 32 * ((x - sp // 8 + 4) % 4)
    )
    index[...] = jnp.where(r < ROWS, r, ROWS + ((INV * kk) % NDEV) * CAP + (r - ROWS) % CAP)

    pl.semaphore_wait(barrier, 10)
    signal(s2, zs)
    for load in loads:
        load.wait()

    pieces = (c * 8 + x, c * 8 + 4 + z)
    for d, dev in zip((1, 2, 3), ys):
        for piece in pieces:
            pltpu.make_async_remote_copy(
                w.at[0, :, piece], w.at[d, :, piece], w_send, w_recv.at[0], device_id=dev, device_id_type=MESH
            ).start()

    lane = lax.broadcasted_iota(jnp.int32, (CAP, NDEV), 1)
    cell = lax.broadcasted_iota(jnp.int32, (CAP, ROWS), 1)

    def gather(j, source):
        def hot(i):
            pp, tt = partner(j * PER + i)
            column = jnp.sum(jnp.where(lane == pp * 4 + tt, ids[...], 0.0), axis=1, keepdims=True)
            return jnp.where(cell == column.astype(jnp.int32), 1.0, 0.0).astype(BF16)

        picked = jnp.concatenate([hot(i) for i in range(PER)], axis=0)
        rows = jnp.dot(picked, source[...], preferred_element_type=F32).astype(BF16)
        send[pl.ds(j * PER, PER)] = rows.reshape(PER, CAP, D)

    def to_raw(k):
        pp, tt = partner(k)
        pltpu.make_async_remote_copy(
            send.at[k], raw.at[k], send_sem, recv_sem.at[k // PER], device_id=(pp, tt), device_id_type=MESH
        ).start()

    def to_table(k):
        pp, tt = partner(k)
        pltpu.make_async_remote_copy(
            send.at[k], table.at[pl.ds(pl.multiple_of(ROWS + k * CAP, CAP), CAP)],
            send_sem, recv_sem.at[k // PER], device_id=(pp, tt), device_id_type=MESH,
        ).start()

    def start(j, put):
        def one(i, _):
            put(j * PER + i)
            return 0

        lax.fori_loop(0, PER, one, 0)

    def raw_chunks(lo, hi):
        def one(j, _):
            gather(j, latent)
            start(j, to_raw)
            return 0

        lax.fori_loop(lo, hi, one, 0)

    gather(0, latent)
    pl.semaphore_wait(s2, 3)
    signal(s3, xs)
    gather(1, latent)
    raw[0] = send[0]
    pl.semaphore_wait(s3, 3)
    signal(s4, [(sib, y)])
    gather(2, latent)
    pl.semaphore_wait(s4, 1)

    def first(k, _):
        to_raw(k)
        return 0

    lax.fori_loop(1, 3 * PER, first, 0)

    pltpu.make_async_copy(w.at[pl.ds(1, 3), :, pl.ds(0, 2)], w.at[pl.ds(1, 3), :, pl.ds(0, 2)], w_recv.at[0]).wait()
    for piece, line in zip(pieces, (xs, zs)):
        for dev in line:
            part = w.at[pl.ds(1, 3), :, piece]
            pltpu.make_async_remote_copy(part, part, w_send, w_recv.at[1], device_id=dev, device_id_type=MESH).start()
    raw_chunks(3, 6)
    pltpu.make_async_copy(w.at[pl.ds(1, 3), :, pl.ds(0, 6)], w.at[pl.ds(1, 3), :, pl.ds(0, 6)], w_recv.at[1]).wait()
    half = w.at[pl.ds(1, 3), :, pl.ds(c * 8, 8)]
    pltpu.make_async_remote_copy(half, half, w_send, w_recv.at[2], device_id=(sib, y), device_id_type=MESH).start()
    raw_chunks(6, RAW)
    pltpu.make_async_copy(w.at[pl.ds(1, 3), :, pl.ds(0, 8)], w.at[pl.ds(1, 3), :, pl.ds(0, 8)], w_recv.at[2]).wait()

    def own(i, _):
        at = pl.ds(pl.multiple_of(i * CROWS, CROWS), CROWS)
        upd[at] = process(latent[at], gain[...], w)
        return 0

    lax.fori_loop(0, ROWS // CROWS, own, 0)
    keep = pltpu.make_async_copy(upd, table.at[pl.ds(0, ROWS)], out_sem.at[0])
    keep.start()

    def processed(j, _):
        gather(j, upd)
        start(j, to_table)
        return 0

    lax.fori_loop(RAW, CHUNKS, processed, 0)

    def arrived(j, _):
        @pl.when(j == 0)
        def _():
            pltpu.make_async_copy(raw.at[pl.ds(1, PER - 1)], raw.at[pl.ds(1, PER - 1)], recv_sem.at[0]).wait()

        @pl.when(j > 0)
        def _():
            part = raw.at[pl.ds(j * PER, PER)]
            pltpu.make_async_copy(part, part, recv_sem.at[j]).wait()

        at = pl.ds(j * PER, PER)
        raw[at] = process(raw[at].reshape(CROWS, D), gain[...], w).reshape(PER, CAP, D)
        return 0

    lax.fori_loop(0, RAW, arrived, 0)
    outs = pltpu.make_async_copy(
        raw, table.at[pl.ds(ROWS, RAW * CROWS)].reshape(RAW * PER, CAP, D), out_sem.at[1]
    )
    outs.start()

    def late(j, _):
        part = table.at[pl.ds(pl.multiple_of(ROWS + j * CROWS, CROWS), CROWS)]
        pltpu.make_async_copy(part, part, recv_sem.at[j]).wait()
        return 0

    lax.fori_loop(RAW, CHUNKS, late, 0)
    keep.wait()
    outs.wait()
    pltpu.make_async_copy(send.at[pl.ds(0, NDEV - 1)], send.at[pl.ds(0, NDEV - 1)], send_sem).wait()
    for n in (2, 6, 8):
        part = w.at[pl.ds(1, 3), :, pl.ds(0, n)]
        pltpu.make_async_copy(part, part, w_send).wait()


def exchange(latent, gain, w_in, w_out, send_rows, obs_src):
    vmem, any_ = pl.BlockSpec(memory_space=pltpu.VMEM), pl.BlockSpec(memory_space=pl.ANY)
    return pl.pallas_call(
        exchange_kernel,
        out_shape=(
            jax.ShapeDtypeStruct((ROWS + NDEV * CAP, D), BF16),
            jax.ShapeDtypeStruct((OBS // 128, 128), jnp.int32),
        ),
        in_specs=[vmem, vmem, any_, any_, vmem, vmem],
        out_specs=(any_, vmem),
        scratch_shapes=[
            pltpu.VMEM((4, 2, 16, 32, D), BF16),
            pltpu.VMEM((NDEV, CAP, D), BF16),
            pltpu.VMEM((RAW * PER, CAP, D), BF16),
            pltpu.VMEM((ROWS, D), BF16),
            pltpu.VMEM((CAP, NDEV), F32),
            pltpu.SemaphoreType.DMA((2,)),
            pltpu.SemaphoreType.DMA,
            pltpu.SemaphoreType.DMA((3,)),
            pltpu.SemaphoreType.DMA,
            pltpu.SemaphoreType.DMA((CHUNKS,)),
            pltpu.SemaphoreType.DMA((2,)),
            pltpu.SemaphoreType.REGULAR,
            pltpu.SemaphoreType.REGULAR,
            pltpu.SemaphoreType.REGULAR,
        ],
        compiler_params=pltpu.CompilerParams(collective_id=0, has_side_effects=True, vmem_limit_bytes=56 << 20),
        name="exchange",
    )(latent, gain.reshape(1, D), w_in.reshape(16, 32, D), w_out.reshape(16, 32, D), send_rows, obs_src.reshape(OBS // 128, 128))


def decode_kernel(
    index, table, feat, inst, embed, w_dec, w_feat, w_head, latent_out, decoded, tab, picked, w2, sem
):
    step = pl.program_id(0)
    keep = pltpu.make_async_copy(table.at[pl.ds(0, ROWS)], latent_out, sem)

    @pl.when(step == 0)
    def _():
        keep.start()

        def widen(i, _):
            for n in range(4):
                at = pl.ds(pl.multiple_of(i * 256, 256), 256)
                tab[pl.ds(i * 1024 + n, 256, stride=4), :] = table[at, n * 128:(n + 1) * 128].astype(F32)
            return 0

        lax.fori_loop(0, (ROWS + NDEV * CAP) // 256, widen, 0)
        high = embed[...].astype(BF16)
        w2[0:128] = w_feat[...]
        w2[128:160] = high
        w2[160:192] = (embed[...] - high.astype(F32)).astype(BF16)

    def pick(i, _):
        for u in range(16):
            j = i * 16 + u
            row = index[step * BLOCK + j]
            picked[pl.ds(pl.multiple_of(j * 4, 4), 4), :] = tab[pl.ds(pl.multiple_of(row * 4, 4), 4), :]
        return 0

    lax.fori_loop(0, BLOCK // 16, pick, 0)
    rows = jnp.concatenate([picked[pl.ds(n, BLOCK, stride=4), :].astype(BF16) for n in range(4)], axis=1)
    which = lax.broadcasted_iota(jnp.int32, (64, BLOCK), 0) % 32
    hot = jnp.where(which == inst[0], 1.0, 0.0).T.astype(BF16)
    side = jnp.concatenate([feat[...], hot], axis=1)
    total = jnp.zeros((BLOCK, 128), F32)
    for n in range(4):
        at = slice(n * 512, (n + 1) * 512)
        pre = jnp.dot(rows, w_dec[:, at], preferred_element_type=F32) + jnp.dot(
            side, w2[:, at], preferred_element_type=F32
        )
        total = total + jnp.dot(gelu(pre).astype(BF16), w_head[at, :], preferred_element_type=F32)
    decoded[...] = total

    @pl.when(step == OBS // BLOCK - 1)
    def _():
        keep.wait()


def decode(index, table, feat, inst, embed, w_dec, w_feat, w_head):
    whole = lambda a: pl.BlockSpec(a.shape, lambda i, _: (0, 0), pipeline_mode=pl.Buffered(1))
    return pl.pallas_call(
        decode_kernel,
        out_shape=(jax.ShapeDtypeStruct((ROWS, D), BF16), jax.ShapeDtypeStruct((OBS, 128), F32)),
        grid_spec=pltpu.PrefetchScalarGridSpec(
            num_scalar_prefetch=1,
            grid=(OBS // BLOCK,),
            in_specs=[
                whole(table),
                pl.BlockSpec((BLOCK, 128), lambda i, _: (i, 0)),
                pl.BlockSpec((1, 1, BLOCK), lambda i, _: (i, 0, 0)),
                whole(embed), whole(w_dec), whole(w_feat), whole(w_head),
            ],
            out_specs=(pl.BlockSpec(memory_space=pl.ANY), pl.BlockSpec((BLOCK, 128), lambda i, _: (i, 0))),
            scratch_shapes=[
                pltpu.VMEM((4 * (ROWS + NDEV * CAP), 128), F32),
                pltpu.VMEM((4 * BLOCK, 128), F32),
                pltpu.VMEM((192, FF), BF16),
                pltpu.SemaphoreType.DMA,
            ],
        ),
        compiler_params=pltpu.CompilerParams(vmem_limit_bytes=56 << 20, dimension_semantics=("arbitrary",)),
        name="decode",
    )(index, table, feat, inst.reshape(OBS // BLOCK, 1, BLOCK), embed, w_dec, w_feat, w_head)


def local(latent, norm_gain, w_in, w_out, send_rows, obs_src, obs_feat, obs_inst, inst_embed, w_dec, w_feat, w_head):
    table, index = exchange(latent, norm_gain, w_in, w_out, send_rows, obs_src)
    return decode(index.reshape(-1), table, obs_feat, obs_inst, inst_embed, w_dec, w_feat, w_head)


def solution(mesh):
    in_specs = (
        P(("pix", "tp"), None),
        P(),
        P(None, "tp"),
        P("tp", None),
        P(("pix", "tp"), None),
        P(("pix", "tp")),
        P(("pix", "tp"), None),
        P(("pix", "tp")),
        P(),
        P(),
        P(),
        P(),
    )
    out_specs = (P(("pix", "tp"), None), P(("pix", "tp"), None))
    return jax.shard_map(local, mesh=mesh, in_specs=in_specs, out_specs=out_specs, check_vma=False)
```

```python
import jax
import jax.numpy as jnp
from jax import lax
from jax.experimental import pallas as pl
from jax.experimental.pallas import tpu as pltpu
from jax.sharding import PartitionSpec as P

MESH = pl.DeviceIdType.MESH
F32, BF16 = jnp.float32, jnp.bfloat16

ROWS = 1024
D = 512
FF = 2048
CAP = 32
NDEV = 128
PER = 8
CHUNKS = NDEV // PER
CROWS = PER * CAP
MUL, INV = 37, 45
TABLE = ROWS + NDEV * CAP
OBS = 4096
BLOCK = 512
BLOCKS = OBS // BLOCK
EVENTS = CHUNKS + 1
SIDE = 192


def gelu(x):
    u = x * (0.7978845608028654 + 0.035677408136300125 * (x * x))
    h = 0.5 * x
    return h + h * jnp.tanh(u)


def coords():
    p, y = lax.axis_index("pix"), lax.axis_index("tp")
    return p // 8, (p // 2) % 4, p % 2, y


def partner(k):
    x, z, c, y = coords()
    kk = (MUL * k) % NDEV
    dy, dc, dz, dx = kk % 4, (kk // 4) % 2, (kk // 8) % 4, kk // 32
    return ((x + dx) % 4) * 8 + ((z + dz) % 4) * 2 + (c + dc) % 2, (y + dy) % 4


def step_of(block):
    return (5 * block) // 2


def process(rows, gain, wi, wo, inner):
    values = rows.astype(F32)
    center = values - jnp.mean(values, axis=-1, keepdims=True)
    spread = jnp.mean(center * center, axis=-1, keepdims=True)
    normed = (center * lax.rsqrt(spread + 1e-05) * gain).astype(BF16)
    for d in range(4):
        inner[:, d * D:(d + 1) * D] = gelu(
            jnp.dot(normed, wi[d].reshape(D, D), preferred_element_type=F32)
        ).astype(BF16)
    update = jnp.dot(inner[...], wo[...].reshape(FF, D), preferred_element_type=F32)
    return (values + update).astype(BF16)


def widen(tab, start, rows):
    n = rows.shape[0]
    for q in range(4):
        tab[pl.ds(start * 4 + q, n, stride=4), :] = rows[:, q * 128:(q + 1) * 128].astype(F32)


def load_decoder(embed, wall):
    high = embed[...].astype(BF16)
    wall[640:672] = high
    wall[672:704] = (embed[...] - high.astype(F32)).astype(BF16)


def pick_sides(order_s, order_v, feats, sorted_feats, sides):
    def pick(i, _):
        for u in range(16):
            j = i * 16 + u
            sorted_feats[pl.ds(j, 1), :] = feats[pl.ds(order_s[OBS + j], 1), :]
        return 0

    lax.fori_loop(0, OBS // 16, pick, 0)
    which = lax.broadcasted_iota(jnp.int32, (64, BLOCK), 0) % 32

    def fill(b, _):
        at = pl.ds(pl.multiple_of(b * BLOCK, BLOCK), BLOCK)
        inst = order_v[pl.ds(64 + b * (BLOCK // 128), BLOCK // 128), :]
        inst = jnp.concatenate([inst[q:q + 1] for q in range(BLOCK // 128)], axis=1)
        hot = jnp.where(which == inst, 1.0, 0.0).T.astype(BF16)
        sides[at] = jnp.concatenate([sorted_feats[at].astype(BF16), hot], axis=1)
        return 0

    lax.fori_loop(0, BLOCKS, fill, 0)


def decode_block(b, order_s, tab, picked, sides, wall, hidden, head):
    at = pl.ds(pl.multiple_of(b * BLOCK, BLOCK), BLOCK)

    def pick(i, _):
        for u in range(16):
            j = i * 16 + u
            picked[pl.ds(pl.multiple_of(j * 4, 4), 4), :] = tab[pl.ds(order_s[b * BLOCK + j] * 4, 4), :]
        return 0

    lax.fori_loop(0, BLOCK // 16, pick, 0)
    full = jnp.concatenate(
        [picked[pl.ds(q, BLOCK, stride=4), :].astype(BF16) for q in range(4)] + [sides[at]], axis=1
    )
    for n in range(4):
        cols = slice(n * 512, (n + 1) * 512)
        hidden[:, cols] = gelu(jnp.dot(full, wall[:, cols], preferred_element_type=F32)).astype(BF16)
    return jnp.dot(hidden[...], head[...], preferred_element_type=F32)


def lines():
    x, z, c, y = coords()
    xs = [(((x + d) % 4) * 8 + z * 2 + c, y) for d in (1, 2, 3)]
    zs = [(x * 8 + ((z + d) % 4) * 2 + c, y) for d in (1, 2, 3)]
    ys = [(x * 8 + z * 2 + c, (y + 4 - d) % 4) for d in (1, 2, 3)]
    return xs, ys, zs, [(x * 8 + z * 2 + 1 - c, y)]


def signal(sem, who):
    for dev in who:
        pl.semaphore_signal(sem, inc=1, device_id=dev, device_id_type=MESH)


def sort(obs_src, obs_inst, order, acc):
    x, z, c, y = coords()
    r = obs_src[...]
    s = jnp.maximum(r - ROWS, 0) // CAP
    sp, st = s // 4, s % 4
    kk = (
        (y - st + 4) % 4
        + 4 * ((c - sp % 2 + 2) % 2)
        + 8 * ((z - (sp // 2) % 4 + 4) % 4)
        + 32 * ((x - sp // 8 + 4) % 4)
    )
    k = (INV * kk) % NDEV
    place = jnp.where(r < ROWS, r, ROWS + k * CAP + (r - ROWS) % CAP)
    event = jnp.where(r < ROWS, 0, 1 + k // PER)
    marks = [jnp.where(event == e, 1.0, 0.0) for e in range(EVENTS)]
    mark = jnp.concatenate(marks, axis=0).astype(BF16)
    n = 32 * EVENTS
    ahead = lax.broadcasted_iota(jnp.int32, (128, 128), 0) <= lax.broadcasted_iota(jnp.int32, (128, 128), 1)
    within = jnp.dot(mark, jnp.where(ahead, 1.0, 0.0).astype(BF16), preferred_element_type=F32)
    counts = jnp.dot(mark, jnp.ones((128, 128), BF16), preferred_element_type=F32).astype(BF16)
    before = lax.broadcasted_iota(jnp.int32, (n, n), 1) < lax.broadcasted_iota(jnp.int32, (n, n), 0)
    base = jnp.dot(jnp.where(before, 1.0, 0.0).astype(BF16), counts, preferred_element_type=F32)
    where = base + within - 1.0
    position = jnp.zeros((32, 128), F32)
    for e in range(EVENTS):
        position = position + marks[e] * where[e * 32:(e + 1) * 32]
    order[0:32] = place
    order[64:96] = obs_inst[...]
    order[96:128] = position.astype(jnp.int32)
    acc[...] = jnp.zeros_like(acc)
    major = lax.broadcasted_iota(jnp.int32, (32, 128), 0)
    minor = lax.broadcasted_iota(jnp.int32, (128, 128), 0)
    across = lax.broadcasted_iota(jnp.int32, (1, 128), 1)

    def line(i, _):
        to = order[pl.ds(96 + i, 1), :]
        what = order[pl.ds(i, 1), :]
        high = major == to // 128
        loads = (what // 128, what % 128, jnp.zeros((1, 128), jnp.int32) + i, across, order[pl.ds(64 + i, 1), :])
        a = jnp.concatenate([jnp.where(high, v.astype(F32), 0.0) for v in loads], axis=0).astype(BF16)
        b = jnp.where(minor == to % 128, 1.0, 0.0).astype(BF16)
        acc[...] += lax.dot_general(a, b, (((1,), (1,)), ((), ())), preferred_element_type=F32)
        return 0

    lax.fori_loop(0, 32, line, 0)
    order[0:32] = jnp.clip((acc[0:32] * 128.0 + acc[32:64]).astype(jnp.int32), 0, TABLE - 1)
    order[32:64] = jnp.clip((acc[64:96] * 128.0 + acc[96:128]).astype(jnp.int32), 0, OBS - 1)
    order[64:96] = acc[128:160].astype(jnp.int32)


def weights_kernel(w_in, w_out, obs_src, obs_inst, wi, wo, order, acc, w_send, w_recv):
    x, z, c, y = coords()
    xs, ys, zs, sibling = lines()
    barrier = pltpu.get_barrier_semaphore()
    signal(barrier, ys + xs + zs + sibling)
    pl.semaphore_wait(barrier, 10)

    def send(source, dest, phase, d, dev):
        pltpu.make_async_remote_copy(
            source, dest, w_send, w_recv.at[phase, d - 1], device_id=dev, device_id_type=MESH
        ).start()

    def wait(phase, d, n):
        part = wi.at[d - 1, pl.ds(0, 2 * n)]
        pltpu.make_async_copy(part, part, w_recv.at[phase, d - 1]).wait()

    pieces = (c * 8 + x, c * 8 + 4 + z)
    turns = (1, 3, 2)
    for d in turns:
        for piece in pieces:
            for own, ref in ((w_in, wi), (w_out, wo)):
                send(own.at[piece], ref.at[d - 1, piece], 0, d, ys[d - 1])
    sort(obs_src, obs_inst, order, acc)
    for d in turns:
        wait(0, d, 2)
        for n in range(3):
            for piece, line in zip(pieces, (xs, zs)):
                for ref in (wi, wo):
                    send(ref.at[d - 1, piece], ref.at[d - 1, piece], 1, d, line[n])
    for d in turns:
        wait(1, d, 6)
        for ref in (wi, wo):
            half = ref.at[d - 1, pl.ds(c * 8, 8)]
            send(half, half, 2, d, sibling[0])
    for d in turns:
        wait(2, d, 8)
    for n in (2, 6, 8):
        for ref in (wi, wo):
            part = ref.at[pl.ds(0, 3), pl.ds(0, n)]
            pltpu.make_async_copy(part, part, w_send).wait()


def gather_weights(w_in, w_out, obs_src, obs_inst):
    vmem, any_ = pl.BlockSpec(memory_space=pltpu.VMEM), pl.BlockSpec(memory_space=pl.ANY)
    return pl.pallas_call(
        weights_kernel,
        out_shape=(
            jax.ShapeDtypeStruct((3, 16, 32, D), BF16),
            jax.ShapeDtypeStruct((3, 16, 32, D), BF16),
            jax.ShapeDtypeStruct((128, 128), jnp.int32),
        ),
        in_specs=[vmem] * 4,
        out_specs=(any_, any_, vmem),
        scratch_shapes=[
            pltpu.VMEM((160, 128), F32),
            pltpu.SemaphoreType.DMA,
            pltpu.SemaphoreType.DMA((3, 3)),
        ],
        compiler_params=pltpu.CompilerParams(collective_id=0, has_side_effects=True, vmem_limit_bytes=56 << 20),
        name="gather_weights",
    )(w_in.reshape(16, 32, D), w_out.reshape(16, 32, D), obs_src.reshape(32, 128), obs_inst.reshape(32, 128))


def exchange_kernel(
    latent, gain, lists, order_s, order, w_in, w_out, w_in3, w_out3, feat, embed, w_dec, w_feat, w_head,
    table, decoded,
    wi, wo, send, recv, upd, inner, tab, featb, feats, sfeats, picked, sides, wall, hidden, head, emb, dec,
    load_sem, send_sem, recv_sem, out_sem, s2, s3, s4,
):
    xs, ys, zs, sibling = lines()
    barrier = pltpu.get_barrier_semaphore()
    signal(barrier, ys + zs + xs + sibling)
    own_w = [
        pltpu.make_async_copy(w_in, wi.at[0], load_sem.at[0]),
        pltpu.make_async_copy(w_out, wo.at[0], load_sem.at[1]),
        pltpu.make_async_copy(w_in3, wi.at[pl.ds(1, 3)], load_sem.at[7]),
        pltpu.make_async_copy(w_out3, wo.at[pl.ds(1, 3)], load_sem.at[8]),
    ]
    loads = [
        pltpu.make_async_copy(feat, featb, load_sem.at[2]),
        pltpu.make_async_copy(embed, emb, load_sem.at[3]),
        pltpu.make_async_copy(w_dec, wall.at[pl.ds(0, 512)], load_sem.at[4]),
        pltpu.make_async_copy(w_feat, wall.at[pl.ds(512, 128)], load_sem.at[5]),
        pltpu.make_async_copy(w_head, head, load_sem.at[6]),
    ]
    for load in own_w + loads:
        load.start()

    lane = lax.broadcasted_iota(jnp.int32, (CAP, NDEV), 1)
    cell = lax.broadcasted_iota(jnp.int32, (CAP, ROWS), 1)

    def gather(j, source):
        def hot(i):
            pp, tt = partner(j * PER + i)
            column = jnp.sum(jnp.where(lane == pp * 4 + tt, lists[...], 0).astype(F32), axis=1, keepdims=True)
            return jnp.where(cell == column.astype(jnp.int32), 1.0, 0.0).astype(BF16)

        chosen = jnp.concatenate([hot(i) for i in range(PER)], axis=0)
        rows = jnp.dot(chosen, source[...], preferred_element_type=F32).astype(BF16)
        send[pl.ds(j * PER, PER)] = rows.reshape(PER, CAP, D)

    def put(k):
        pltpu.make_async_remote_copy(
            send.at[k], recv.at[k], send_sem, recv_sem.at[k // PER], device_id=partner(k), device_id_type=MESH
        ).start()

    def start(lo, hi):
        def one(k, _):
            put(k)
            return 0

        lax.fori_loop(lo, hi, one, 0)

    def chunks(lo, hi, source):
        def one(j, _):
            gather(j, source)
            start(j * PER, j * PER + PER)
            return 0

        lax.fori_loop(lo, hi, one, 0)

    def own(i, _):
        at = pl.ds(pl.multiple_of(i * CROWS, CROWS), CROWS)
        upd[at] = process(latent[at], gain[...], wi, wo, inner)
        return 0

    pl.semaphore_wait(barrier, 10)
    signal(s2, zs)
    for load in own_w:
        load.wait()
    own(0, 0)
    pl.semaphore_wait(s2, 3)
    signal(s3, xs)
    own(1, 0)
    pl.semaphore_wait(s3, 3)
    signal(s4, sibling)
    own(2, 0)
    own(3, 0)
    keep = pltpu.make_async_copy(upd, table.at[pl.ds(0, ROWS)], out_sem.at[0])
    keep.start()
    gather(0, upd)
    recv[0] = send[0]
    pl.semaphore_wait(s4, 1)
    start(1, PER)
    chunks(1, CHUNKS, upd)
    for load in loads:
        load.wait()
    load_decoder(emb, wall)
    feats[...] = featb[...].astype(F32)
    pick_sides(order_s, order, feats, sfeats, sides)

    def spread_own(i, _):
        widen(tab, i * CROWS, upd[pl.ds(pl.multiple_of(i * CROWS, CROWS), CROWS)])
        return 0

    lax.fori_loop(0, ROWS // CROWS, spread_own, 0)

    rest = pltpu.make_async_copy(recv, table.at[pl.ds(ROWS, NDEV * CAP)].reshape(NDEV, CAP, D), out_sem.at[2])

    def step(s, _):
        j = s - 1

        @pl.when(j == 0)
        def _():
            pltpu.make_async_copy(recv.at[pl.ds(1, PER - 1)], recv.at[pl.ds(1, PER - 1)], recv_sem.at[0]).wait()

        @pl.when(jnp.logical_and(j > 0, j < CHUNKS))
        def _():
            part = recv.at[pl.ds(j * PER, PER)]
            pltpu.make_async_copy(part, part, recv_sem.at[j]).wait()

        @pl.when(jnp.logical_and(j >= 0, j < CHUNKS))
        def _():
            widen(tab, ROWS + j * CROWS, recv[pl.ds(j * PER, PER)].reshape(CROWS, D))

        @pl.when(s == EVENTS)
        def _():
            rest.start()

        b = (2 * s + 1) // 5

        @pl.when(step_of(b) == s)
        def _():
            at = pl.ds(pl.multiple_of(b * BLOCK, BLOCK), BLOCK)
            dec[at] = decode_block(b, order_s, tab, picked, sides, wall, hidden, head)
            pltpu.make_async_copy(dec.at[at], decoded.at[at], out_sem.at[1]).start()

        return 0

    lax.fori_loop(0, EVENTS + 1, step, 0)
    rest.wait()
    keep.wait()
    pltpu.make_async_copy(dec, decoded, out_sem.at[1]).wait()
    pltpu.make_async_copy(send.at[pl.ds(0, NDEV - 1)], send.at[pl.ds(0, NDEV - 1)], send_sem).wait()


def exchange(latent, gain, send_rows, order, w_in, w_out, w_in3, w_out3, feat, embed, w_dec, w_feat, w_head):
    vmem, any_ = pl.BlockSpec(memory_space=pltpu.VMEM), pl.BlockSpec(memory_space=pl.ANY)
    return pl.pallas_call(
        exchange_kernel,
        out_shape=(
            jax.ShapeDtypeStruct((TABLE, D), BF16),
            jax.ShapeDtypeStruct((OBS, 128), F32),
        ),
        in_specs=[vmem, vmem, vmem, pl.BlockSpec(memory_space=pltpu.SMEM), vmem] + [any_] * 9,
        out_specs=(any_, any_),
        scratch_shapes=[
            pltpu.VMEM((4, 16, 32, D), BF16),
            pltpu.VMEM((4, 16, 32, D), BF16),
            pltpu.VMEM((NDEV, CAP, D), BF16),
            pltpu.VMEM((NDEV, CAP, D), BF16),
            pltpu.VMEM((ROWS, D), BF16),
            pltpu.VMEM((CROWS, FF), BF16),
            pltpu.VMEM((4 * TABLE + 8, 128), F32),
            pltpu.VMEM((OBS, 128), BF16),
            pltpu.VMEM((OBS, 128), F32),
            pltpu.VMEM((OBS, 128), F32),
            pltpu.VMEM((4 * BLOCK + 8, 128), F32),
            pltpu.VMEM((OBS, SIDE), BF16),
            pltpu.VMEM((512 + SIDE, FF), BF16),
            pltpu.VMEM((BLOCK, FF), BF16),
            pltpu.VMEM((FF, 128), BF16),
            pltpu.VMEM((32, FF), F32),
            pltpu.VMEM((OBS, 128), F32),
            pltpu.SemaphoreType.DMA((9,)),
            pltpu.SemaphoreType.DMA,
            pltpu.SemaphoreType.DMA((CHUNKS,)),
            pltpu.SemaphoreType.DMA((3,)),
            pltpu.SemaphoreType.REGULAR,
            pltpu.SemaphoreType.REGULAR,
            pltpu.SemaphoreType.REGULAR,
        ],
        compiler_params=pltpu.CompilerParams(collective_id=1, has_side_effects=True, vmem_limit_bytes=60 << 20),
        name="exchange",
    )(
        latent, gain.reshape(1, D), send_rows.T, order.reshape(-1), order, w_in.reshape(16, 32, D),
        w_out.reshape(16, 32, D), w_in3, w_out3, feat, embed, w_dec, w_feat, w_head,
    )


def finish_kernel(
    order_s, order_v, dec_in, table, feat, embed, w_dec, w_feat, w_head, latent_out, decoded,
    dec, lat, tabb, tab, featb, feats, sfeats, picked, sides, wall, hidden, head, emb, sem, load_sem,
):
    i = pl.program_id(0)
    keep = pltpu.make_async_copy(lat, latent_out, sem.at[2])

    @pl.when(i == 0)
    def _():
        first = pltpu.make_async_copy(table.at[pl.ds(0, ROWS)], lat, sem.at[0])
        second = pltpu.make_async_copy(dec_in, dec, sem.at[1])
        second.start()
        first.start()
        first.wait()
        keep.start()
        second.wait()

        def missed(b):
            last = order_s[b * BLOCK + BLOCK - 1]
            return jnp.where(last < ROWS, 0, 1 + (last - ROWS) // CROWS) > step_of(b)

        any_missed = missed(0)
        for b in range(1, BLOCKS):
            any_missed = jnp.logical_or(any_missed, missed(b))

        @pl.when(any_missed)
        def _():
            loads = [
                pltpu.make_async_copy(feat, featb, load_sem.at[0]),
                pltpu.make_async_copy(embed, emb, load_sem.at[1]),
                pltpu.make_async_copy(w_dec, wall.at[pl.ds(0, 512)], load_sem.at[2]),
                pltpu.make_async_copy(w_feat, wall.at[pl.ds(512, 128)], load_sem.at[3]),
                pltpu.make_async_copy(w_head, head, load_sem.at[4]),
                pltpu.make_async_copy(table, tabb, load_sem.at[5]),
            ]
            for load in loads:
                load.start()
            for load in loads:
                load.wait()
            load_decoder(emb, wall)
            feats[...] = featb[...].astype(F32)
            pick_sides(order_s, order_v, feats, sfeats, sides)

            def spread(n, _):
                widen(tab, n * CROWS, tabb[pl.ds(pl.multiple_of(n * CROWS, CROWS), CROWS)])
                return 0

            lax.fori_loop(0, TABLE // CROWS, spread, 0)

            def again(b, _):
                @pl.when(missed(b))
                def _():
                    dec[pl.ds(pl.multiple_of(b * BLOCK, BLOCK), BLOCK)] = decode_block(
                        b, order_s, tab, picked, sides, wall, hidden, head
                    )

                return 0

            lax.fori_loop(0, BLOCKS, again, 0)

    def back(n, _):
        for u in range(32):
            j = n * 32 + u
            decoded[pl.ds(j, 1), :] = dec[pl.ds(order_s[3 * OBS + i * BLOCK + j], 1), :]
        return 0

    lax.fori_loop(0, BLOCK // 32, back, 0)

    @pl.when(i == BLOCKS - 1)
    def _():
        keep.wait()


def finish(order, dec, table, feat, embed, w_dec, w_feat, w_head):
    any_ = pl.BlockSpec(memory_space=pl.ANY)
    return pl.pallas_call(
        finish_kernel,
        out_shape=(jax.ShapeDtypeStruct((ROWS, D), BF16), jax.ShapeDtypeStruct((OBS, 128), F32)),
        grid_spec=pltpu.PrefetchScalarGridSpec(
            num_scalar_prefetch=1,
            grid=(BLOCKS,),
            in_specs=[pl.BlockSpec((128, 128), lambda i, _: (0, 0))] + [any_] * 7,
            out_specs=(any_, pl.BlockSpec((BLOCK, 128), lambda i, _: (i, 0))),
            scratch_shapes=[
                pltpu.VMEM((OBS, 128), F32),
                pltpu.VMEM((ROWS, D), BF16),
                pltpu.VMEM((TABLE, D), BF16),
                pltpu.VMEM((4 * TABLE + 8, 128), F32),
                pltpu.VMEM((OBS, 128), BF16),
                pltpu.VMEM((OBS, 128), F32),
                pltpu.VMEM((OBS, 128), F32),
                pltpu.VMEM((4 * BLOCK + 8, 128), F32),
                pltpu.VMEM((OBS, SIDE), BF16),
                pltpu.VMEM((512 + SIDE, FF), BF16),
                pltpu.VMEM((BLOCK, FF), BF16),
                pltpu.VMEM((FF, 128), BF16),
                pltpu.VMEM((32, FF), F32),
                pltpu.SemaphoreType.DMA((3,)),
                pltpu.SemaphoreType.DMA((6,)),
            ],
        ),
        compiler_params=pltpu.CompilerParams(vmem_limit_bytes=56 << 20, dimension_semantics=("arbitrary",)),
        name="finish",
    )(order.reshape(-1), order, dec, table, feat, embed, w_dec, w_feat, w_head)


def local(latent, norm_gain, w_in, w_out, send_rows, obs_src, obs_feat, obs_inst, inst_embed, w_dec, w_feat, w_head):
    w_in3, w_out3, order = gather_weights(w_in, w_out, obs_src, obs_inst)
    table, dec = exchange(
        latent, norm_gain, send_rows, order, w_in, w_out, w_in3, w_out3, obs_feat, inst_embed, w_dec, w_feat, w_head
    )
    return finish(order, dec, table, obs_feat, inst_embed, w_dec, w_feat, w_head)


def solution(mesh):
    in_specs = (
        P(("pix", "tp"), None),
        P(),
        P(None, "tp"),
        P("tp", None),
        P(("pix", "tp"), None),
        P(("pix", "tp")),
        P(("pix", "tp"), None),
        P(("pix", "tp")),
        P(),
        P(),
        P(),
        P(),
    )
    out_specs = (P(("pix", "tp"), None), P(("pix", "tp"), None))
    return jax.shard_map(local, mesh=mesh, in_specs=in_specs, out_specs=out_specs, check_vma=False)
```

```python
import jax
import jax.numpy as jnp
from jax import lax
from jax.experimental import pallas as pl
from jax.experimental.pallas import tpu as pltpu
from jax.sharding import PartitionSpec as P

MESH = pl.DeviceIdType.MESH
F32, BF16 = jnp.float32, jnp.bfloat16

ROWS = 1024
D = 512
FF = 2048
CAP = 32
NDEV = 128
PER = 8
CHUNKS = NDEV // PER
CROWS = PER * CAP
MUL, INV = 37, 45
TABLE = ROWS + NDEV * CAP
OBS = 4096
BLOCK = 512
BLOCKS = OBS // BLOCK
EVENTS = CHUNKS + 1
OUT = 1024
SIDE = 192


def gelu(x):
    u = x * (0.7978845608028654 + 0.035677408136300125 * (x * x))
    h = 0.5 * x
    return h + h * jnp.tanh(u)


def coords():
    p, y = lax.axis_index("pix"), lax.axis_index("tp")
    return p // 8, (p // 2) % 4, p % 2, y


def partner(k):
    x, z, c, y = coords()
    kk = (MUL * k) % NDEV
    dy, dc, dz, dx = kk % 4, (kk // 4) % 2, (kk // 8) % 4, kk // 32
    return ((x + dx) % 4) * 8 + ((z + dz) % 4) * 2 + (c + dc) % 2, (y + dy) % 4


def step_of(block):
    return (5 * block) // 2


def normalise(rows, gain):
    values = rows.astype(F32)
    center = values - jnp.mean(values, axis=-1, keepdims=True)
    spread = jnp.mean(center * center, axis=-1, keepdims=True)
    return (center * lax.rsqrt(spread + 1e-05) * gain).astype(BF16)


def widen(tab, start, rows):
    n = rows.shape[0]
    for q in range(4):
        tab[pl.ds(start * 4 + q, n, stride=4), :] = rows[:, q * 128:(q + 1) * 128].astype(F32)


def load_decoder(embed, wall):
    high = embed[...].astype(BF16)
    wall[640:672] = high
    wall[672:704] = (embed[...] - high.astype(F32)).astype(BF16)


def pick_sides(order_s, order_v, feats, sorted_feats, sides):
    def pick(i, _):
        for u in range(16):
            j = i * 16 + u
            sorted_feats[pl.ds(j, 1), :] = feats[pl.ds(order_s[OBS + j], 1), :]
        return 0

    lax.fori_loop(0, OBS // 16, pick, 0)
    which = lax.broadcasted_iota(jnp.int32, (64, BLOCK), 0) % 32

    def fill(b, _):
        at = pl.ds(pl.multiple_of(b * BLOCK, BLOCK), BLOCK)
        inst = order_v[pl.ds(64 + b * (BLOCK // 128), BLOCK // 128), :]
        inst = jnp.concatenate([inst[q:q + 1] for q in range(BLOCK // 128)], axis=1)
        hot = jnp.where(which == inst, 1.0, 0.0).T.astype(BF16)
        sides[at] = jnp.concatenate([sorted_feats[at].astype(BF16), hot], axis=1)
        return 0

    lax.fori_loop(0, BLOCKS, fill, 0)


def decode_block(b, order_s, tab, picked, sides, wall, hidden, head):
    at = pl.ds(pl.multiple_of(b * BLOCK, BLOCK), BLOCK)

    def pick(i, _):
        for u in range(16):
            j = i * 16 + u
            picked[pl.ds(pl.multiple_of(j * 4, 4), 4), :] = tab[pl.ds(order_s[b * BLOCK + j] * 4, 4), :]
        return 0

    lax.fori_loop(0, BLOCK // 16, pick, 0)
    full = jnp.concatenate(
        [picked[pl.ds(q, BLOCK, stride=4), :].astype(BF16) for q in range(4)] + [sides[at]], axis=1
    )
    for n in range(4):
        cols = slice(n * 512, (n + 1) * 512)
        hidden[:, cols] = gelu(jnp.dot(full, wall[:, cols], preferred_element_type=F32)).astype(BF16)
    return jnp.dot(hidden[...], head[...], preferred_element_type=F32)


def lines():
    x, z, c, y = coords()
    ys = [(x * 8 + z * 2 + c, (y + 4 - d) % 4) for d in (1, 2, 3)]
    zs = [(x * 8 + ((z + d) % 4) * 2 + c, y) for d in (1, 2, 3)]
    xs = [(((x + d) % 4) * 8 + z * 2 + c, y) for d in (1, 2, 3)]
    others = [(((x + d) % 4) * 8 + z * 2 + 1 - c, y) for d in (0, 1, 2, 3)]
    return ys, zs, xs, others


def signal(sem, who):
    for dev in who:
        pl.semaphore_signal(sem, inc=1, device_id=dev, device_id_type=MESH)


def sort(obs_src, obs_inst, order, place, acc):
    x, z, c, y = coords()
    r = obs_src[...]
    s = jnp.maximum(r - ROWS, 0) // CAP
    sp, st = s // 4, s % 4
    kk = (
        (y - st + 4) % 4
        + 4 * ((c - sp % 2 + 2) % 2)
        + 8 * ((z - (sp // 2) % 4 + 4) % 4)
        + 32 * ((x - sp // 8 + 4) % 4)
    )
    k = (INV * kk) % NDEV
    row = jnp.where(r < ROWS, r, ROWS + k * CAP + (r - ROWS) % CAP)
    event = jnp.where(r < ROWS, 0, 1 + k // PER)
    marks = [jnp.where(event == e, 1.0, 0.0) for e in range(EVENTS)]
    mark = jnp.concatenate(marks, axis=0).astype(BF16)
    n = 32 * EVENTS
    ahead = lax.broadcasted_iota(jnp.int32, (128, 128), 0) <= lax.broadcasted_iota(jnp.int32, (128, 128), 1)
    within = jnp.dot(mark, jnp.where(ahead, 1.0, 0.0).astype(BF16), preferred_element_type=F32)
    counts = jnp.dot(mark, jnp.ones((128, 128), BF16), preferred_element_type=F32).astype(BF16)
    before = lax.broadcasted_iota(jnp.int32, (n, n), 1) < lax.broadcasted_iota(jnp.int32, (n, n), 0)
    base = jnp.dot(jnp.where(before, 1.0, 0.0).astype(BF16), counts, preferred_element_type=F32)
    where = base + within - 1.0
    position = jnp.zeros((32, 128), F32)
    for e in range(EVENTS):
        position = position + marks[e] * where[e * 32:(e + 1) * 32]
    order[0:32] = row
    order[64:96] = obs_inst[...]
    place[0:32] = position.astype(jnp.int32)
    acc[...] = jnp.zeros_like(acc)
    major = lax.broadcasted_iota(jnp.int32, (32, 128), 0)
    minor = lax.broadcasted_iota(jnp.int32, (128, 128), 0)
    across = lax.broadcasted_iota(jnp.int32, (1, 128), 1)

    def line(i, _):
        to = place[pl.ds(i, 1), :]
        what = order[pl.ds(i, 1), :]
        high = major == to // 128
        loads = (what // 128, what % 128, jnp.zeros((1, 128), jnp.int32) + i, across, order[pl.ds(64 + i, 1), :])
        a = jnp.concatenate([jnp.where(high, v.astype(F32), 0.0) for v in loads], axis=0).astype(BF16)
        b = jnp.where(minor == to % 128, 1.0, 0.0).astype(BF16)
        acc[...] += lax.dot_general(a, b, (((1,), (1,)), ((), ())), preferred_element_type=F32)
        return 0

    lax.fori_loop(0, 32, line, 0)
    order[0:32] = jnp.clip((acc[0:32] * 128.0 + acc[32:64]).astype(jnp.int32), 0, TABLE - 1)
    order[32:64] = jnp.clip((acc[64:96] * 128.0 + acc[96:128]).astype(jnp.int32), 0, OBS - 1)
    order[64:96] = acc[128:160].astype(jnp.int32)
    for b in range(BLOCKS):
        last = (b + 1) * (BLOCK // 128) - 1
        place[32 + b:33 + b] = order[last:last + 1]


def process_kernel(
    latent, gain, w_in, w_out, obs_src, obs_inst, upd, order, place,
    wi, wo, normed, total, acc, w_send, w_recv,
):
    x, z, c, y = coords()
    ys, zs, xs, others = lines()
    barrier = pltpu.get_barrier_semaphore()
    signal(barrier, ys + xs + zs + others[:1])

    def prepare(i, _):
        at = pl.ds(pl.multiple_of(i * 256, 256), 256)
        normed[at] = normalise(latent[at], gain[...])
        total[at] = latent[at].astype(F32)
        return 0

    lax.fori_loop(0, ROWS // 256, prepare, 0)
    pl.semaphore_wait(barrier, 10)

    def send(source, dest, phase, d, dev):
        pltpu.make_async_remote_copy(
            source, dest, w_send, w_recv.at[phase, d - 1], device_id=dev, device_id_type=MESH
        ).start()

    def wait(phase, d, n):
        part = wi.at[d - 1, pl.ds(0, 2 * n)]
        pltpu.make_async_copy(part, part, w_recv.at[phase, d - 1]).wait()

    def shard(first, second):
        def rows(i, _):
            at = pl.ds(pl.multiple_of(i * 512, 512), 512)
            inner = gelu(jnp.dot(normed[at], first, preferred_element_type=F32)).astype(BF16)
            total[at] += jnp.dot(inner, second, preferred_element_type=F32)
            return 0

        lax.fori_loop(0, ROWS // 512, rows, 0)

    pieces = (c * 8 + x, c * 8 + 4 + z)
    turns = (1, 3, 2)
    for d in turns:
        for piece in pieces:
            for own, ref in ((w_in, wi), (w_out, wo)):
                send(own.at[piece], ref.at[d - 1, piece], 0, d, ys[d - 1])
    shard(w_in[...].reshape(D, D), w_out[...].reshape(D, D))
    for d in turns:
        wait(0, d, 2)
        for n in range(3):
            for piece, line in zip(pieces, (xs, zs)):
                for ref in (wi, wo):
                    send(ref.at[d - 1, piece], ref.at[d - 1, piece], 1, d, line[n])
    sort(obs_src, obs_inst, order, place, acc)
    for d in turns:
        wait(1, d, 6)
        for ref in (wi, wo):
            half = ref.at[d - 1, pl.ds(c * 8, 8)]
            send(half, half, 2, d, others[0])
    for d in turns:
        wait(2, d, 8)
        shard(wi[d - 1].reshape(D, D), wo[d - 1].reshape(D, D))

    upd[...] = total[...].astype(BF16)
    for n in (2, 6, 8):
        for ref in (wi, wo):
            part = ref.at[pl.ds(0, 3), pl.ds(0, n)]
            pltpu.make_async_copy(part, part, w_send).wait()


def process(latent, gain, w_in, w_out, obs_src, obs_inst):
    vmem = pl.BlockSpec(memory_space=pltpu.VMEM)
    return pl.pallas_call(
        process_kernel,
        out_shape=(
            jax.ShapeDtypeStruct((ROWS, D), BF16),
            jax.ShapeDtypeStruct((96, 128), jnp.int32),
            jax.ShapeDtypeStruct((32 + BLOCKS, 128), jnp.int32),
        ),
        in_specs=[vmem] * 6,
        out_specs=(vmem,) * 3,
        scratch_shapes=[
            pltpu.VMEM((3, 16, 32, D), BF16),
            pltpu.VMEM((3, 16, 32, D), BF16),
            pltpu.VMEM((ROWS, D), BF16),
            pltpu.VMEM((ROWS, D), F32),
            pltpu.VMEM((160, 128), F32),
            pltpu.SemaphoreType.DMA,
            pltpu.SemaphoreType.DMA((3, 3)),
        ],
        compiler_params=pltpu.CompilerParams(collective_id=0, has_side_effects=True, vmem_limit_bytes=56 << 20),
        name="process",
    )(
        latent, gain.reshape(1, D), w_in.reshape(16, 32, D), w_out.reshape(16, 32, D),
        obs_src.reshape(32, 128), obs_inst.reshape(32, 128),
    )


def exchange_kernel(
    upd, lists, order_s, order, feat, embed, w_dec, w_feat, w_head, table, decoded,
    send, recv, tab, featb, feats, sfeats, picked, sides, wall, hidden, head, emb, dec,
    load_sem, send_sem, recv_sem, out_sem, s2, s3,
):
    ys, zs, xs, others = lines()
    barrier = pltpu.get_barrier_semaphore()
    signal(barrier, ys + zs + xs + others)
    loads = [
        pltpu.make_async_copy(feat, featb, load_sem.at[0]),
        pltpu.make_async_copy(embed, emb, load_sem.at[1]),
        pltpu.make_async_copy(w_dec, wall.at[pl.ds(0, 512)], load_sem.at[2]),
        pltpu.make_async_copy(w_feat, wall.at[pl.ds(512, 128)], load_sem.at[3]),
        pltpu.make_async_copy(w_head, head, load_sem.at[4]),
    ]
    for load in loads:
        load.start()

    lane = lax.broadcasted_iota(jnp.int32, (CAP, NDEV), 1)
    cell = lax.broadcasted_iota(jnp.int32, (CAP, ROWS), 1)

    def gather(j, source):
        def hot(i):
            pp, tt = partner(j * PER + i)
            column = jnp.sum(jnp.where(lane == pp * 4 + tt, lists[...], 0).astype(F32), axis=1, keepdims=True)
            return jnp.where(cell == column.astype(jnp.int32), 1.0, 0.0).astype(BF16)

        chosen = jnp.concatenate([hot(i) for i in range(PER)], axis=0)
        rows = jnp.dot(chosen, source[...], preferred_element_type=F32).astype(BF16)
        send[pl.ds(j * PER, PER)] = rows.reshape(PER, CAP, D)

    def put(k):
        pltpu.make_async_remote_copy(
            send.at[k], recv.at[k], send_sem, recv_sem.at[k // PER], device_id=partner(k), device_id_type=MESH
        ).start()

    def start(lo, hi):
        def one(k, _):
            put(k)
            return 0

        lax.fori_loop(lo, hi, one, 0)

    def chunks(lo, hi, source):
        def one(j, _):
            gather(j, source)
            start(j * PER, j * PER + PER)
            return 0

        lax.fori_loop(lo, hi, one, 0)

    gather(0, upd)
    recv[0] = send[0]
    pl.semaphore_wait(barrier, 13)
    signal(s2, zs)
    gather(1, upd)
    pl.semaphore_wait(s2, 3)
    signal(s3, xs + others)
    gather(2, upd)
    pl.semaphore_wait(s3, 7)
    start(1, 3 * PER)
    chunks(3, CHUNKS, upd)
    for load in loads:
        load.wait()
    load_decoder(emb, wall)
    feats[...] = featb[...].astype(F32)
    pick_sides(order_s, order, feats, sfeats, sides)

    def spread_own(i, _):
        widen(tab, i * CROWS, upd[pl.ds(pl.multiple_of(i * CROWS, CROWS), CROWS)])
        return 0

    lax.fori_loop(0, ROWS // CROWS, spread_own, 0)

    rest = pltpu.make_async_copy(recv, table, out_sem.at[0])

    def step(s, _):
        j = s - 1

        @pl.when(j == 0)
        def _():
            pltpu.make_async_copy(recv.at[pl.ds(1, PER - 1)], recv.at[pl.ds(1, PER - 1)], recv_sem.at[0]).wait()

        @pl.when(jnp.logical_and(j > 0, j < CHUNKS))
        def _():
            part = recv.at[pl.ds(j * PER, PER)]
            pltpu.make_async_copy(part, part, recv_sem.at[j]).wait()

        @pl.when(jnp.logical_and(j >= 0, j < CHUNKS))
        def _():
            widen(tab, ROWS + j * CROWS, recv[pl.ds(j * PER, PER)].reshape(CROWS, D))

        @pl.when(s == EVENTS)
        def _():
            rest.start()

        b = (2 * s + 1) // 5

        @pl.when(step_of(b) == s)
        def _():
            at = pl.ds(pl.multiple_of(b * BLOCK, BLOCK), BLOCK)
            dec[at] = decode_block(b, order_s, tab, picked, sides, wall, hidden, head)
            pltpu.make_async_copy(dec.at[at], decoded.at[at], out_sem.at[1]).start()

        return 0

    lax.fori_loop(0, EVENTS + 1, step, 0)
    rest.wait()
    pltpu.make_async_copy(dec, decoded, out_sem.at[1]).wait()
    pltpu.make_async_copy(send.at[pl.ds(0, NDEV - 1)], send.at[pl.ds(0, NDEV - 1)], send_sem).wait()


def exchange(upd, send_rows, order, feat, embed, w_dec, w_feat, w_head):
    vmem, any_ = pl.BlockSpec(memory_space=pltpu.VMEM), pl.BlockSpec(memory_space=pl.ANY)
    return pl.pallas_call(
        exchange_kernel,
        out_shape=(
            jax.ShapeDtypeStruct((NDEV, CAP, D), BF16),
            jax.ShapeDtypeStruct((OBS, 128), F32),
        ),
        in_specs=[vmem, vmem, pl.BlockSpec(memory_space=pltpu.SMEM), vmem] + [any_] * 5,
        out_specs=(any_, any_),
        scratch_shapes=[
            pltpu.VMEM((NDEV, CAP, D), BF16),
            pltpu.VMEM((NDEV, CAP, D), BF16),
            pltpu.VMEM((4 * TABLE + 8, 128), F32),
            pltpu.VMEM((OBS, 128), BF16),
            pltpu.VMEM((OBS, 128), F32),
            pltpu.VMEM((OBS, 128), F32),
            pltpu.VMEM((4 * BLOCK + 8, 128), F32),
            pltpu.VMEM((OBS, SIDE), BF16),
            pltpu.VMEM((512 + SIDE, FF), BF16),
            pltpu.VMEM((BLOCK, FF), BF16),
            pltpu.VMEM((FF, 128), BF16),
            pltpu.VMEM((32, FF), F32),
            pltpu.VMEM((OBS, 128), F32),
            pltpu.SemaphoreType.DMA((5,)),
            pltpu.SemaphoreType.DMA,
            pltpu.SemaphoreType.DMA((CHUNKS,)),
            pltpu.SemaphoreType.DMA((2,)),
            pltpu.SemaphoreType.REGULAR,
            pltpu.SemaphoreType.REGULAR,
        ],
        compiler_params=pltpu.CompilerParams(collective_id=1, has_side_effects=True, vmem_limit_bytes=60 << 20),
        name="exchange",
    )(upd, send_rows.T, order.reshape(-1), order, feat, embed, w_dec, w_feat, w_head)


def finish_kernel(
    place, order, upd, dec_in, table, feat, embed, w_dec, w_feat, w_head, latent_out, decoded,
    dec, lat, tabb, tab, featb, feats, sfeats, picked, sides, wall, hidden, head, emb, order_s, order_v, sem, load_sem,
):
    i = pl.program_id(0)
    keep = pltpu.make_async_copy(lat, latent_out, sem.at[2])

    @pl.when(i == 0)
    def _():
        first = pltpu.make_async_copy(upd, lat, sem.at[0])
        second = pltpu.make_async_copy(dec_in, dec, sem.at[1])
        second.start()
        first.start()
        first.wait()
        keep.start()
        second.wait()

        def missed(b):
            last = place[(32 + b) * 128 + 127]
            return jnp.where(last < ROWS, 0, 1 + (last - ROWS) // CROWS) > step_of(b)

        any_missed = missed(0)
        for b in range(1, BLOCKS):
            any_missed = jnp.logical_or(any_missed, missed(b))

        @pl.when(any_missed)
        def _():
            loads = [
                pltpu.make_async_copy(feat, featb, load_sem.at[0]),
                pltpu.make_async_copy(embed, emb, load_sem.at[1]),
                pltpu.make_async_copy(w_dec, wall.at[pl.ds(0, 512)], load_sem.at[2]),
                pltpu.make_async_copy(w_feat, wall.at[pl.ds(512, 128)], load_sem.at[3]),
                pltpu.make_async_copy(w_head, head, load_sem.at[4]),
                pltpu.make_async_copy(table, tabb, load_sem.at[5]),
                pltpu.make_async_copy(order, order_v, load_sem.at[6]),
            ]
            for load in loads:
                load.start()
            for load in loads:
                load.wait()
            load_decoder(emb, wall)
            feats[...] = featb[...].astype(F32)

            def to_scalar(n, _):
                to = order_s.at[pl.ds(pl.multiple_of(n * 128, 128), 128)]
                copy = pltpu.make_async_copy(order_v.at[n], to, load_sem.at[7])
                copy.start()
                copy.wait()
                return 0

            lax.fori_loop(0, 64, to_scalar, 0)
            pick_sides(order_s, order_v, feats, sfeats, sides)

            def spread_own(n, _):
                widen(tab, n * CROWS, lat[pl.ds(pl.multiple_of(n * CROWS, CROWS), CROWS)])
                return 0

            lax.fori_loop(0, ROWS // CROWS, spread_own, 0)

            def spread(n, _):
                widen(tab, ROWS + n * CROWS, tabb[pl.ds(n * PER, PER)].reshape(CROWS, D))
                return 0

            lax.fori_loop(0, CHUNKS, spread, 0)

            def again(b, _):
                @pl.when(missed(b))
                def _():
                    dec[pl.ds(pl.multiple_of(b * BLOCK, BLOCK), BLOCK)] = decode_block(
                        b, order_s, tab, picked, sides, wall, hidden, head
                    )

                return 0

            lax.fori_loop(0, BLOCKS, again, 0)

    def back(n, _):
        for u in range(32):
            j = n * 32 + u
            decoded[pl.ds(j, 1), :] = dec[pl.ds(place[i * OUT + j], 1), :]
        return 0

    lax.fori_loop(0, OUT // 32, back, 0)

    @pl.when(i == OBS // OUT - 1)
    def _():
        keep.wait()


def finish(place, order, upd, dec, table, feat, embed, w_dec, w_feat, w_head):
    any_ = pl.BlockSpec(memory_space=pl.ANY)
    return pl.pallas_call(
        finish_kernel,
        out_shape=(jax.ShapeDtypeStruct((ROWS, D), BF16), jax.ShapeDtypeStruct((OBS, 128), F32)),
        grid_spec=pltpu.PrefetchScalarGridSpec(
            num_scalar_prefetch=1,
            grid=(OBS // OUT,),
            in_specs=[any_] * 9,
            out_specs=(any_, pl.BlockSpec((OUT, 128), lambda i, _: (i, 0))),
            scratch_shapes=[
                pltpu.VMEM((OBS, 128), F32),
                pltpu.VMEM((ROWS, D), BF16),
                pltpu.VMEM((NDEV, CAP, D), BF16),
                pltpu.VMEM((4 * TABLE + 8, 128), F32),
                pltpu.VMEM((OBS, 128), BF16),
                pltpu.VMEM((OBS, 128), F32),
                pltpu.VMEM((OBS, 128), F32),
                pltpu.VMEM((4 * BLOCK + 8, 128), F32),
                pltpu.VMEM((OBS, SIDE), BF16),
                pltpu.VMEM((512 + SIDE, FF), BF16),
                pltpu.VMEM((BLOCK, FF), BF16),
                pltpu.VMEM((FF, 128), BF16),
                pltpu.VMEM((32, FF), F32),
                pltpu.SMEM((2 * OBS,), jnp.int32),
                pltpu.VMEM((96, 128), jnp.int32),
                pltpu.SemaphoreType.DMA((3,)),
                pltpu.SemaphoreType.DMA((8,)),
            ],
        ),
        compiler_params=pltpu.CompilerParams(vmem_limit_bytes=56 << 20, dimension_semantics=("arbitrary",)),
        name="finish",
    )(place.reshape(-1), order, upd, dec, table, feat, embed, w_dec, w_feat, w_head)


def local(latent, norm_gain, w_in, w_out, send_rows, obs_src, obs_feat, obs_inst, inst_embed, w_dec, w_feat, w_head):
    upd, order, place = process(latent, norm_gain, w_in, w_out, obs_src, obs_inst)
    table, dec = exchange(upd, send_rows, order, obs_feat, inst_embed, w_dec, w_feat, w_head)
    return finish(place, order, upd, dec, table, obs_feat, inst_embed, w_dec, w_feat, w_head)


def solution(mesh):
    in_specs = (
        P(("pix", "tp"), None),
        P(),
        P(None, "tp"),
        P("tp", None),
        P(("pix", "tp"), None),
        P(("pix", "tp")),
        P(("pix", "tp"), None),
        P(("pix", "tp")),
        P(),
        P(),
        P(),
        P(),
    )
    out_specs = (P(("pix", "tp"), None), P(("pix", "tp"), None))
    return jax.shard_map(local, mesh=mesh, in_specs=in_specs, out_specs=out_specs, check_vma=False)
```

```python
import jax
import jax.numpy as jnp
from jax import lax
from jax.experimental import pallas as pl
from jax.experimental.pallas import tpu as pltpu
from jax.sharding import PartitionSpec as P

MESH = pl.DeviceIdType.MESH
F32, BF16 = jnp.float32, jnp.bfloat16

ROWS = 1024
D = 512
FF = 2048
CAP = 32
NDEV = 128
PER = 8
CHUNKS = NDEV // PER
CROWS = PER * CAP
MUL, INV = 37, 45
TABLE = ROWS + NDEV * CAP
OBS = 4096
BLOCK = 512
BLOCKS = OBS // BLOCK
EVENTS = CHUNKS + 1
EARLY = 6
LATE = OBS - EARLY * BLOCK
SIDE = 192


def gelu(x):
    u = x * (0.7978845608028654 + 0.035677408136300125 * (x * x))
    h = 0.5 * x
    return h + h * jnp.tanh(u)


def coords():
    p, y = lax.axis_index("pix"), lax.axis_index("tp")
    return p // 8, (p // 2) % 4, p % 2, y


def partner(k):
    x, z, c, y = coords()
    kk = (MUL * k) % NDEV
    dy, dc, dz, dx = kk % 4, (kk // 4) % 2, (kk // 8) % 4, kk // 32
    return ((x + dx) % 4) * 8 + ((z + dz) % 4) * 2 + (c + dc) % 2, (y + dy) % 4


def step_of(block):
    return (5 * block) // 2 - block // 6 + block // 7


def normalise(rows, gain):
    values = rows.astype(F32)
    center = values - jnp.mean(values, axis=-1, keepdims=True)
    spread = jnp.mean(center * center, axis=-1, keepdims=True)
    return (center * lax.rsqrt(spread + 1e-05) * gain).astype(BF16)


def widen(tab, start, rows):
    n = rows.shape[0]
    for q in range(4):
        tab[pl.ds(start * 4 + q, n, stride=4), :] = rows[:, q * 128:(q + 1) * 128].astype(F32)


def load_decoder(embed, wall):
    high = embed[...].astype(BF16)
    wall[640:672] = high
    wall[672:704] = (embed[...] - high.astype(F32)).astype(BF16)


def pick_sides(order_s, order_v, feats, sorted_feats, sides):
    def pick(i, _):
        for u in range(16):
            j = i * 16 + u
            sorted_feats[pl.ds(j, 1), :] = feats[pl.ds(order_s[OBS + j], 1), :]
        return 0

    lax.fori_loop(0, OBS // 16, pick, 0)
    which = lax.broadcasted_iota(jnp.int32, (64, BLOCK), 0) % 32

    def fill(b, _):
        at = pl.ds(pl.multiple_of(b * BLOCK, BLOCK), BLOCK)
        inst = order_v[pl.ds(64 + b * (BLOCK // 128), BLOCK // 128), :]
        inst = jnp.concatenate([inst[q:q + 1] for q in range(BLOCK // 128)], axis=1)
        hot = jnp.where(which == inst, 1.0, 0.0).T.astype(BF16)
        sides[at] = jnp.concatenate([sorted_feats[at].astype(BF16), hot], axis=1)
        return 0

    lax.fori_loop(0, BLOCKS, fill, 0)


def decode_block(b, order_s, tab, picked, sides, wall, hidden, head):
    at = pl.ds(pl.multiple_of(b * BLOCK, BLOCK), BLOCK)

    def pick(i, _):
        for u in range(16):
            j = i * 16 + u
            picked[pl.ds(pl.multiple_of(j * 4, 4), 4), :] = tab[pl.ds(order_s[b * BLOCK + j] * 4, 4), :]
        return 0

    lax.fori_loop(0, BLOCK // 16, pick, 0)
    full = jnp.concatenate(
        [picked[pl.ds(q, BLOCK, stride=4), :].astype(BF16) for q in range(4)] + [sides[at]], axis=1
    )
    for n in range(4):
        cols = slice(n * 512, (n + 1) * 512)
        hidden[:, cols] = gelu(jnp.dot(full, wall[:, cols], preferred_element_type=F32)).astype(BF16)
    return jnp.dot(hidden[...], head[...], preferred_element_type=F32)


def lines():
    x, z, c, y = coords()
    ys = [(x * 8 + z * 2 + c, (y + 4 - d) % 4) for d in (1, 2, 3)]
    zs = [(x * 8 + ((z + d) % 4) * 2 + c, y) for d in (1, 2, 3)]
    xs = [(((x + d) % 4) * 8 + z * 2 + c, y) for d in (1, 2, 3)]
    others = [(((x + d) % 4) * 8 + z * 2 + 1 - c, y) for d in (0, 1, 2, 3)]
    return ys, zs, xs, others


def signal(sem, who):
    for dev in who:
        pl.semaphore_signal(sem, inc=1, device_id=dev, device_id_type=MESH)


def sort(obs_src, obs_inst, order, place, acc):
    x, z, c, y = coords()
    r = obs_src[...]
    s = jnp.maximum(r - ROWS, 0) // CAP
    sp, st = s // 4, s % 4
    kk = (
        (y - st + 4) % 4
        + 4 * ((c - sp % 2 + 2) % 2)
        + 8 * ((z - (sp // 2) % 4 + 4) % 4)
        + 32 * ((x - sp // 8 + 4) % 4)
    )
    k = (INV * kk) % NDEV
    row = jnp.where(r < ROWS, r, ROWS + k * CAP + (r - ROWS) % CAP)
    event = jnp.where(r < ROWS, 0, 1 + k // PER)
    marks = [jnp.where(event == e, 1.0, 0.0) for e in range(EVENTS)]
    mark = jnp.concatenate(marks, axis=0).astype(BF16)
    n = 32 * EVENTS
    ahead = lax.broadcasted_iota(jnp.int32, (128, 128), 0) <= lax.broadcasted_iota(jnp.int32, (128, 128), 1)
    within = jnp.dot(mark, jnp.where(ahead, 1.0, 0.0).astype(BF16), preferred_element_type=F32)
    counts = jnp.dot(mark, jnp.ones((128, 128), BF16), preferred_element_type=F32).astype(BF16)
    before = lax.broadcasted_iota(jnp.int32, (n, n), 1) < lax.broadcasted_iota(jnp.int32, (n, n), 0)
    base = jnp.dot(jnp.where(before, 1.0, 0.0).astype(BF16), counts, preferred_element_type=F32)
    where = base + within - 1.0
    position = jnp.zeros((32, 128), F32)
    for e in range(EVENTS):
        position = position + marks[e] * where[e * 32:(e + 1) * 32]
    order[0:32] = row
    order[64:96] = obs_inst[...]
    place[0:32] = position.astype(jnp.int32)
    acc[...] = jnp.zeros_like(acc)
    major = lax.broadcasted_iota(jnp.int32, (32, 128), 0)
    minor = lax.broadcasted_iota(jnp.int32, (128, 128), 0)
    across = lax.broadcasted_iota(jnp.int32, (1, 128), 1)

    def line(i, _):
        to = place[pl.ds(i, 1), :]
        what = order[pl.ds(i, 1), :]
        high = major == to // 128
        loads = (what // 128, what % 128, jnp.zeros((1, 128), jnp.int32) + i, across, order[pl.ds(64 + i, 1), :])
        a = jnp.concatenate([jnp.where(high, v.astype(F32), 0.0) for v in loads], axis=0).astype(BF16)
        b = jnp.where(minor == to % 128, 1.0, 0.0).astype(BF16)
        acc[...] += lax.dot_general(a, b, (((1,), (1,)), ((), ())), preferred_element_type=F32)
        return 0

    lax.fori_loop(0, 32, line, 0)
    order[0:32] = jnp.clip((acc[0:32] * 128.0 + acc[32:64]).astype(jnp.int32), 0, TABLE - 1)
    order[32:64] = jnp.clip((acc[64:96] * 128.0 + acc[96:128]).astype(jnp.int32), 0, OBS - 1)
    order[64:96] = acc[128:160].astype(jnp.int32)
    for b in range(BLOCKS):
        last = (b + 1) * (BLOCK // 128) - 1
        place[32 + b:33 + b] = order[last:last + 1]
    place[40:48] = order[32 + EARLY * (BLOCK // 128):64]


def process_kernel(
    latent_h, gain, w_in_h, w_out_h, obs_src, obs_inst, upd, order, place,
    latent, w_in, w_out, wi, wo, normed, total, acc, load_sem, w_send, w_recv,
):
    x, z, c, y = coords()
    ys, zs, xs, others = lines()
    barrier = pltpu.get_barrier_semaphore()
    loads = [
        pltpu.make_async_copy(source, ref, load_sem.at[n])
        for n, (source, ref) in enumerate(((latent_h, latent), (w_in_h, w_in), (w_out_h, w_out)))
    ]
    for load in loads:
        load.start()
    signal(barrier, ys + xs + zs + others[:1])
    loads[0].wait()

    def prepare(i, _):
        at = pl.ds(pl.multiple_of(i * 256, 256), 256)
        normed[at] = normalise(latent[at], gain[...])
        total[at] = latent[at].astype(F32)
        return 0

    lax.fori_loop(0, ROWS // 256, prepare, 0)
    for load in loads[1:]:
        load.wait()
    pl.semaphore_wait(barrier, 10)

    def send(source, dest, phase, d, dev):
        pltpu.make_async_remote_copy(
            source, dest, w_send, w_recv.at[phase, d - 1], device_id=dev, device_id_type=MESH
        ).start()

    def wait(phase, d, n):
        part = wi.at[d - 1, pl.ds(0, 2 * n)]
        pltpu.make_async_copy(part, part, w_recv.at[phase, d - 1]).wait()

    def shard(first, second):
        def rows(i, _):
            at = pl.ds(pl.multiple_of(i * 512, 512), 512)
            inner = gelu(jnp.dot(normed[at], first, preferred_element_type=F32)).astype(BF16)
            total[at] += jnp.dot(inner, second, preferred_element_type=F32)
            return 0

        lax.fori_loop(0, ROWS // 512, rows, 0)

    pieces = (c * 8 + x, c * 8 + 4 + z)
    turns = (1, 3, 2)
    for d in turns:
        for piece in pieces:
            for own, ref in ((w_in, wi), (w_out, wo)):
                send(own.at[piece], ref.at[d - 1, piece], 0, d, ys[d - 1])
    shard(w_in[...].reshape(D, D), w_out[...].reshape(D, D))
    for d in turns:
        wait(0, d, 2)
        for n in range(3):
            for piece, line in zip(pieces, (xs, zs)):
                for ref in (wi, wo):
                    send(ref.at[d - 1, piece], ref.at[d - 1, piece], 1, d, line[n])
    sort(obs_src, obs_inst, order, place, acc)
    for d in turns:
        wait(1, d, 6)
        for ref in (wi, wo):
            half = ref.at[d - 1, pl.ds(c * 8, 8)]
            send(half, half, 2, d, others[0])
    for d in turns:
        wait(2, d, 8)
        shard(wi[d - 1].reshape(D, D), wo[d - 1].reshape(D, D))

    upd[...] = total[...].astype(BF16)
    for n in (2, 6, 8):
        for ref in (wi, wo):
            part = ref.at[pl.ds(0, 3), pl.ds(0, n)]
            pltpu.make_async_copy(part, part, w_send).wait()


def process(latent, gain, w_in, w_out, obs_src, obs_inst):
    vmem, any_ = pl.BlockSpec(memory_space=pltpu.VMEM), pl.BlockSpec(memory_space=pl.ANY)
    return pl.pallas_call(
        process_kernel,
        out_shape=(
            jax.ShapeDtypeStruct((ROWS, D), BF16),
            jax.ShapeDtypeStruct((96, 128), jnp.int32),
            jax.ShapeDtypeStruct((48, 128), jnp.int32),
        ),
        in_specs=[any_, vmem, any_, any_, vmem, vmem],
        out_specs=(vmem,) * 3,
        scratch_shapes=[
            pltpu.VMEM((ROWS, D), BF16),
            pltpu.VMEM((16, 32, D), BF16),
            pltpu.VMEM((16, 32, D), BF16),
            pltpu.VMEM((3, 16, 32, D), BF16),
            pltpu.VMEM((3, 16, 32, D), BF16),
            pltpu.VMEM((ROWS, D), BF16),
            pltpu.VMEM((ROWS, D), F32),
            pltpu.VMEM((160, 128), F32),
            pltpu.SemaphoreType.DMA((3,)),
            pltpu.SemaphoreType.DMA,
            pltpu.SemaphoreType.DMA((3, 3)),
        ],
        compiler_params=pltpu.CompilerParams(collective_id=0, has_side_effects=True, vmem_limit_bytes=56 << 20),
        name="process",
    )(
        latent, gain.reshape(1, D), w_in.reshape(16, 32, D), w_out.reshape(16, 32, D),
        obs_src.reshape(32, 128), obs_inst.reshape(32, 128),
    )


def exchange_kernel(
    upd_h, lists, order_h, order_vh, place_h, feat, embed, w_dec, w_feat, w_head, table, natural, late,
    upd, order_s, order, place_s,
    send, recv, tab, featb, feats, sfeats, picked, sides, wall, hidden, head, emb, dec, nat,
    load_sem, send_sem, recv_sem, out_sem, s2, s3,
):
    ys, zs, xs, others = lines()
    barrier = pltpu.get_barrier_semaphore()
    signal(barrier, ys + zs + xs + others)
    loads = [
        pltpu.make_async_copy(feat, featb, load_sem.at[0]),
        pltpu.make_async_copy(embed, emb, load_sem.at[1]),
        pltpu.make_async_copy(w_dec, wall.at[pl.ds(0, 512)], load_sem.at[2]),
        pltpu.make_async_copy(w_feat, wall.at[pl.ds(512, 128)], load_sem.at[3]),
        pltpu.make_async_copy(w_head, head, load_sem.at[4]),
        pltpu.make_async_copy(order_h, order_s, load_sem.at[5]),
        pltpu.make_async_copy(order_vh, order, load_sem.at[6]),
        pltpu.make_async_copy(place_h, place_s, load_sem.at[7]),
    ]
    rows_in = pltpu.make_async_copy(upd_h, upd, load_sem.at[8])
    rows_in.start()
    for load in loads:
        load.start()

    lane = lax.broadcasted_iota(jnp.int32, (CAP, NDEV), 1)
    cell = lax.broadcasted_iota(jnp.int32, (CAP, ROWS), 1)

    def gather(j, source):
        def hot(i):
            pp, tt = partner(j * PER + i)
            column = jnp.sum(jnp.where(lane == pp * 4 + tt, lists[...], 0).astype(F32), axis=1, keepdims=True)
            return jnp.where(cell == column.astype(jnp.int32), 1.0, 0.0).astype(BF16)

        chosen = jnp.concatenate([hot(i) for i in range(PER)], axis=0)
        rows = jnp.dot(chosen, source[...], preferred_element_type=F32).astype(BF16)
        send[pl.ds(j * PER, PER)] = rows.reshape(PER, CAP, D)

    def put(k):
        pltpu.make_async_remote_copy(
            send.at[k], recv.at[k], send_sem, recv_sem.at[k // PER], device_id=partner(k), device_id_type=MESH
        ).start()

    def start(lo, hi):
        def one(k, _):
            put(k)
            return 0

        lax.fori_loop(lo, hi, one, 0)

    def chunks(lo, hi, source):
        def one(j, _):
            gather(j, source)
            start(j * PER, j * PER + PER)
            return 0

        lax.fori_loop(lo, hi, one, 0)

    rows_in.wait()
    gather(0, upd)
    recv[0] = send[0]
    pl.semaphore_wait(barrier, 13)
    signal(s2, zs)
    gather(1, upd)
    pl.semaphore_wait(s2, 3)
    signal(s3, xs + others)
    gather(2, upd)
    pl.semaphore_wait(s3, 7)
    start(1, 3 * PER)
    chunks(3, CHUNKS, upd)
    for load in loads:
        load.wait()
    load_decoder(emb, wall)
    feats[...] = featb[...].astype(F32)
    pick_sides(order_s, order, feats, sfeats, sides)

    def spread_own(i, _):
        widen(tab, i * CROWS, upd[pl.ds(pl.multiple_of(i * CROWS, CROWS), CROWS)])
        return 0

    lax.fori_loop(0, ROWS // CROWS, spread_own, 0)

    rest = pltpu.make_async_copy(recv, table, out_sem.at[0])
    nat_out = pltpu.make_async_copy(nat, natural, out_sem.at[1])

    def step(s, _):
        j = s - 1

        @pl.when(j == 0)
        def _():
            pltpu.make_async_copy(recv.at[pl.ds(1, PER - 1)], recv.at[pl.ds(1, PER - 1)], recv_sem.at[0]).wait()

        @pl.when(jnp.logical_and(j > 0, j < CHUNKS))
        def _():
            part = recv.at[pl.ds(j * PER, PER)]
            pltpu.make_async_copy(part, part, recv_sem.at[j]).wait()

        @pl.when(jnp.logical_and(j >= 0, j < CHUNKS))
        def _():
            widen(tab, ROWS + j * CROWS, recv[pl.ds(j * PER, PER)].reshape(CROWS, D))

        @pl.when(s == EVENTS)
        def _():
            rest.start()

        b = (2 * s + 1) // 5 + s // 14 - s // 15

        @pl.when(step_of(b) == s)
        def _():
            at = pl.ds(pl.multiple_of(b * BLOCK, BLOCK), BLOCK)
            dec[at] = decode_block(b, order_s, tab, picked, sides, wall, hidden, head)

        @pl.when(s == step_of(EARLY - 1) + 1)
        def _():
            def back(n, _):
                for u in range(64):
                    j = n * 64 + u
                    nat[pl.ds(j, 1), :] = dec[pl.ds(place_s[j], 1), :]
                return 0

            lax.fori_loop(0, OBS // 64, back, 0)
            nat_out.start()

        return 0

    lax.fori_loop(0, EVENTS + 1, step, 0)
    last = pltpu.make_async_copy(dec.at[pl.ds(EARLY * BLOCK, LATE)], late, out_sem.at[2])
    last.start()
    rest.wait()
    nat_out.wait()
    last.wait()
    pltpu.make_async_copy(send.at[pl.ds(0, NDEV - 1)], send.at[pl.ds(0, NDEV - 1)], send_sem).wait()


def exchange(upd, send_rows, order, place, feat, embed, w_dec, w_feat, w_head):
    vmem, any_ = pl.BlockSpec(memory_space=pltpu.VMEM), pl.BlockSpec(memory_space=pl.ANY)
    return pl.pallas_call(
        exchange_kernel,
        out_shape=(
            jax.ShapeDtypeStruct((NDEV, CAP, D), BF16),
            jax.ShapeDtypeStruct((OBS, 128), F32),
            jax.ShapeDtypeStruct((LATE, 128), F32),
        ),
        in_specs=[any_, vmem] + [any_] * 8,
        out_specs=(any_, any_, any_),
        scratch_shapes=[
            pltpu.VMEM((ROWS, D), BF16),
            pltpu.SMEM((96 * 128,), jnp.int32),
            pltpu.VMEM((96, 128), jnp.int32),
            pltpu.SMEM((48 * 128,), jnp.int32),
            pltpu.VMEM((NDEV, CAP, D), BF16),
            pltpu.VMEM((NDEV, CAP, D), BF16),
            pltpu.VMEM((4 * TABLE + 8, 128), F32),
            pltpu.VMEM((OBS, 128), BF16),
            pltpu.VMEM((OBS, 128), F32),
            pltpu.VMEM((OBS, 128), F32),
            pltpu.VMEM((4 * BLOCK + 8, 128), F32),
            pltpu.VMEM((OBS, SIDE), BF16),
            pltpu.VMEM((512 + SIDE, FF), BF16),
            pltpu.VMEM((BLOCK, FF), BF16),
            pltpu.VMEM((FF, 128), BF16),
            pltpu.VMEM((32, FF), F32),
            pltpu.VMEM((OBS, 128), F32),
            pltpu.VMEM((OBS, 128), F32),
            pltpu.SemaphoreType.DMA((9,)),
            pltpu.SemaphoreType.DMA,
            pltpu.SemaphoreType.DMA((CHUNKS,)),
            pltpu.SemaphoreType.DMA((3,)),
            pltpu.SemaphoreType.REGULAR,
            pltpu.SemaphoreType.REGULAR,
        ],
        compiler_params=pltpu.CompilerParams(collective_id=1, has_side_effects=True, vmem_limit_bytes=60 << 20),
        name="exchange",
    )(upd, send_rows.T, order.reshape(-1), order, place.reshape(-1), feat, embed, w_dec, w_feat, w_head)


def finish_kernel(
    place, order, order_h, upd, natural, late, table, feat, embed, w_dec, w_feat, w_head, latent_out, decoded,
    buf, tail, lat, tabb, tab, featb, feats, sfeats, picked, sides, wall, hidden, head, emb, order_s, order_v, sem, load_sem,
):
    ins = [
        pltpu.make_async_copy(natural, buf, sem.at[1]),
        pltpu.make_async_copy(late, tail, sem.at[2]),
        pltpu.make_async_copy(upd, lat, sem.at[0]),
    ]
    for copy in ins:
        copy.start()
    for copy in ins:
        copy.wait()
    keep = pltpu.make_async_copy(lat, latent_out, sem.at[3])
    keep.start()

    def scatter(numbers, start, n):
        def move(i, _):
            for u in range(64):
                j = i * 64 + u
                buf[pl.ds(numbers[start + j], 1), :] = tail[pl.ds(j, 1), :]
            return 0

        lax.fori_loop(0, n // 64, move, 0)

    scatter(place, 40 * 128, LATE)

    def missed(b):
        last = place[(32 + b) * 128 + 127]
        return jnp.where(last < ROWS, 0, 1 + (last - ROWS) // CROWS) > step_of(b)

    any_missed = missed(0)
    for b in range(1, BLOCKS):
        any_missed = jnp.logical_or(any_missed, missed(b))

    @pl.when(any_missed)
    def _():
        loads = [
            pltpu.make_async_copy(feat, featb, load_sem.at[0]),
            pltpu.make_async_copy(embed, emb, load_sem.at[1]),
            pltpu.make_async_copy(w_dec, wall.at[pl.ds(0, 512)], load_sem.at[2]),
            pltpu.make_async_copy(w_feat, wall.at[pl.ds(512, 128)], load_sem.at[3]),
            pltpu.make_async_copy(w_head, head, load_sem.at[4]),
            pltpu.make_async_copy(table, tabb, load_sem.at[5]),
            pltpu.make_async_copy(order, order_v, load_sem.at[6]),
            pltpu.make_async_copy(order_h, order_s, load_sem.at[7]),
        ]
        for load in loads:
            load.start()
        for load in loads:
            load.wait()
        load_decoder(emb, wall)
        feats[...] = featb[...].astype(F32)
        pick_sides(order_s, order_v, feats, sfeats, sides)

        def spread_own(n, _):
            widen(tab, n * CROWS, lat[pl.ds(pl.multiple_of(n * CROWS, CROWS), CROWS)])
            return 0

        lax.fori_loop(0, ROWS // CROWS, spread_own, 0)

        def spread(n, _):
            widen(tab, ROWS + n * CROWS, tabb[pl.ds(n * PER, PER)].reshape(CROWS, D))
            return 0

        lax.fori_loop(0, CHUNKS, spread, 0)

        def again(b, _):
            @pl.when(missed(b))
            def _():
                tail[0:BLOCK] = decode_block(b, order_s, tab, picked, sides, wall, hidden, head)
                scatter(order_s, OBS + b * BLOCK, BLOCK)

            return 0

        lax.fori_loop(0, BLOCKS, again, 0)

    done = pltpu.make_async_copy(buf, decoded, sem.at[4])
    done.start()
    done.wait()
    keep.wait()


def finish(place, order, upd, natural, late, table, feat, embed, w_dec, w_feat, w_head):
    any_ = pl.BlockSpec(memory_space=pl.ANY)
    return pl.pallas_call(
        finish_kernel,
        out_shape=(jax.ShapeDtypeStruct((ROWS, D), BF16), jax.ShapeDtypeStruct((OBS, 128), F32)),
        grid_spec=pltpu.PrefetchScalarGridSpec(
            num_scalar_prefetch=1,
            grid=(1,),
            in_specs=[any_] * 11,
            out_specs=(any_, any_),
            scratch_shapes=[
                pltpu.VMEM((OBS, 128), F32),
                pltpu.VMEM((LATE, 128), F32),
                pltpu.VMEM((ROWS, D), BF16),
                pltpu.VMEM((NDEV, CAP, D), BF16),
                pltpu.VMEM((4 * TABLE + 8, 128), F32),
                pltpu.VMEM((OBS, 128), BF16),
                pltpu.VMEM((OBS, 128), F32),
                pltpu.VMEM((OBS, 128), F32),
                pltpu.VMEM((4 * BLOCK + 8, 128), F32),
                pltpu.VMEM((OBS, SIDE), BF16),
                pltpu.VMEM((512 + SIDE, FF), BF16),
                pltpu.VMEM((BLOCK, FF), BF16),
                pltpu.VMEM((FF, 128), BF16),
                pltpu.VMEM((32, FF), F32),
                pltpu.SMEM((96 * 128,), jnp.int32),
                pltpu.VMEM((96, 128), jnp.int32),
                pltpu.SemaphoreType.DMA((5,)),
                pltpu.SemaphoreType.DMA((8,)),
            ],
        ),
        compiler_params=pltpu.CompilerParams(vmem_limit_bytes=56 << 20, dimension_semantics=("arbitrary",)),
        name="finish",
    )(place.reshape(-1), order, order.reshape(-1), upd, natural, late, table, feat, embed, w_dec, w_feat, w_head)


def local(latent, norm_gain, w_in, w_out, send_rows, obs_src, obs_feat, obs_inst, inst_embed, w_dec, w_feat, w_head):
    upd, order, place = process(latent, norm_gain, w_in, w_out, obs_src, obs_inst)
    table, natural, late = exchange(upd, send_rows, order, place, obs_feat, inst_embed, w_dec, w_feat, w_head)
    return finish(place, order, upd, natural, late, table, obs_feat, inst_embed, w_dec, w_feat, w_head)


def solution(mesh):
    in_specs = (
        P(("pix", "tp"), None),
        P(),
        P(None, "tp"),
        P("tp", None),
        P(("pix", "tp"), None),
        P(("pix", "tp")),
        P(("pix", "tp"), None),
        P(("pix", "tp")),
        P(),
        P(),
        P(),
        P(),
    )
    out_specs = (P(("pix", "tp"), None), P(("pix", "tp"), None))
    return jax.shard_map(local, mesh=mesh, in_specs=in_specs, out_specs=out_specs, check_vma=False)
```

```python
import jax
import jax.numpy as jnp
from jax import lax
from jax.experimental import pallas as pl
from jax.experimental.pallas import tpu as pltpu
from jax.sharding import PartitionSpec as P

MESH = pl.DeviceIdType.MESH
F32, BF16 = jnp.float32, jnp.bfloat16

ROWS = 1024
D = 512
FF = 2048
CAP = 32
NDEV = 128
PER = 8
CHUNKS = NDEV // PER
CROWS = PER * CAP
MUL, INV = 11, 35
TABLE = ROWS + NDEV * CAP
OBS = 4096
BLOCK = 512
BLOCKS = OBS // BLOCK
EVENTS = CHUNKS + 1
EARLY = 6
LATE = OBS - EARLY * BLOCK
SIDE = 192


def gelu(x):
    u = x * (0.7978845608028654 + 0.035677408136300125 * (x * x))
    h = 0.5 * x
    return h + h * jnp.tanh(u)


def coords():
    p, y = lax.axis_index("pix"), lax.axis_index("tp")
    return p // 8, (p // 2) % 4, p % 2, y


def partner(k):
    x, z, c, y = coords()
    kk = (MUL * k) % NDEV
    dy, dc, dz, dx = kk % 4, (kk // 4) % 2, (kk // 8) % 4, kk // 32
    return ((x + dx) % 4) * 8 + ((z + dz) % 4) * 2 + (c + dc) % 2, (y + dy) % 4


def step_of(block):
    return (5 * block) // 2 - block // 6 + block // 7


def normalise(rows, gain):
    values = rows.astype(F32)
    center = values - jnp.mean(values, axis=-1, keepdims=True)
    spread = jnp.mean(center * center, axis=-1, keepdims=True)
    return (center * lax.rsqrt(spread + 1e-05) * gain).astype(BF16)


def widen(tab, start, rows):
    n = rows.shape[0]
    for q in range(4):
        tab[pl.ds(start * 4 + q, n, stride=4), :] = rows[:, q * 128:(q + 1) * 128].astype(F32)


def load_decoder(embed, wall):
    high = embed[...].astype(BF16)
    wall[640:672] = high
    wall[672:704] = (embed[...] - high.astype(F32)).astype(BF16)


def pick_sides(order_s, order_v, feats, sorted_feats, sides):
    def pick(i, _):
        for u in range(16):
            j = i * 16 + u
            sorted_feats[pl.ds(j, 1), :] = feats[pl.ds(order_s[OBS + j], 1), :]
        return 0

    lax.fori_loop(0, OBS // 16, pick, 0)
    which = lax.broadcasted_iota(jnp.int32, (64, BLOCK), 0) % 32

    def fill(b, _):
        at = pl.ds(pl.multiple_of(b * BLOCK, BLOCK), BLOCK)
        inst = order_v[pl.ds(64 + b * (BLOCK // 128), BLOCK // 128), :]
        inst = jnp.concatenate([inst[q:q + 1] for q in range(BLOCK // 128)], axis=1)
        hot = jnp.where(which == inst, 1.0, 0.0).T.astype(BF16)
        sides[at] = jnp.concatenate([sorted_feats[at].astype(BF16), hot], axis=1)
        return 0

    lax.fori_loop(0, BLOCKS, fill, 0)


def decode_block(b, order_s, tab, picked, sides, wall, hidden, head):
    at = pl.ds(pl.multiple_of(b * BLOCK, BLOCK), BLOCK)

    def pick(i, _):
        for u in range(16):
            j = i * 16 + u
            picked[pl.ds(pl.multiple_of(j * 4, 4), 4), :] = tab[pl.ds(order_s[b * BLOCK + j] * 4, 4), :]
        return 0

    lax.fori_loop(0, BLOCK // 16, pick, 0)
    full = jnp.concatenate(
        [picked[pl.ds(q, BLOCK, stride=4), :].astype(BF16) for q in range(4)] + [sides[at]], axis=1
    )
    for n in range(4):
        cols = slice(n * 512, (n + 1) * 512)
        hidden[:, cols] = gelu(jnp.dot(full, wall[:, cols], preferred_element_type=F32)).astype(BF16)
    return jnp.dot(hidden[...], head[...], preferred_element_type=F32)


def lines():
    x, z, c, y = coords()
    ys = [(x * 8 + z * 2 + c, (y + 4 - d) % 4) for d in (1, 2, 3)]
    zs = [(x * 8 + ((z + d) % 4) * 2 + c, y) for d in (1, 2, 3)]
    xs = [(((x + d) % 4) * 8 + z * 2 + c, y) for d in (1, 2, 3)]
    others = [(((x + d) % 4) * 8 + z * 2 + 1 - c, y) for d in (0, 1, 2, 3)]
    return ys, zs, xs, others


def signal(sem, who):
    for dev in who:
        pl.semaphore_signal(sem, inc=1, device_id=dev, device_id_type=MESH)


def sort(obs_src, obs_inst, order, place, acc):
    x, z, c, y = coords()
    r = obs_src[...]
    s = jnp.maximum(r - ROWS, 0) // CAP
    sp, st = s // 4, s % 4
    kk = (
        (y - st + 4) % 4
        + 4 * ((c - sp % 2 + 2) % 2)
        + 8 * ((z - (sp // 2) % 4 + 4) % 4)
        + 32 * ((x - sp // 8 + 4) % 4)
    )
    k = (INV * kk) % NDEV
    row = jnp.where(r < ROWS, r, ROWS + k * CAP + (r - ROWS) % CAP)
    event = jnp.where(r < ROWS, 0, 1 + k // PER)
    marks = [jnp.where(event == e, 1.0, 0.0) for e in range(EVENTS)]
    mark = jnp.concatenate(marks, axis=0).astype(BF16)
    n = 32 * EVENTS
    ahead = lax.broadcasted_iota(jnp.int32, (128, 128), 0) <= lax.broadcasted_iota(jnp.int32, (128, 128), 1)
    within = jnp.dot(mark, jnp.where(ahead, 1.0, 0.0).astype(BF16), preferred_element_type=F32)
    counts = jnp.dot(mark, jnp.ones((128, 128), BF16), preferred_element_type=F32).astype(BF16)
    before = lax.broadcasted_iota(jnp.int32, (n, n), 1) < lax.broadcasted_iota(jnp.int32, (n, n), 0)
    base = jnp.dot(jnp.where(before, 1.0, 0.0).astype(BF16), counts, preferred_element_type=F32)
    where = base + within - 1.0
    position = jnp.zeros((32, 128), F32)
    for e in range(EVENTS):
        position = position + marks[e] * where[e * 32:(e + 1) * 32]
    order[0:32] = row
    order[64:96] = obs_inst[...]
    place[0:32] = position.astype(jnp.int32)
    acc[...] = jnp.zeros_like(acc)
    major = lax.broadcasted_iota(jnp.int32, (32, 128), 0)
    minor = lax.broadcasted_iota(jnp.int32, (128, 128), 0)
    across = lax.broadcasted_iota(jnp.int32, (1, 128), 1)

    def line(i, _):
        to = place[pl.ds(i, 1), :]
        what = order[pl.ds(i, 1), :]
        high = major == to // 128
        loads = (what // 128, what % 128, jnp.zeros((1, 128), jnp.int32) + i, across, order[pl.ds(64 + i, 1), :])
        a = jnp.concatenate([jnp.where(high, v.astype(F32), 0.0) for v in loads], axis=0).astype(BF16)
        b = jnp.where(minor == to % 128, 1.0, 0.0).astype(BF16)
        acc[...] += lax.dot_general(a, b, (((1,), (1,)), ((), ())), preferred_element_type=F32)
        return 0

    lax.fori_loop(0, 32, line, 0)
    order[0:32] = jnp.clip((acc[0:32] * 128.0 + acc[32:64]).astype(jnp.int32), 0, TABLE - 1)
    order[32:64] = jnp.clip((acc[64:96] * 128.0 + acc[96:128]).astype(jnp.int32), 0, OBS - 1)
    order[64:96] = acc[128:160].astype(jnp.int32)
    for b in range(BLOCKS):
        last = (b + 1) * (BLOCK // 128) - 1
        place[32 + b:33 + b] = order[last:last + 1]
    place[40:48] = order[32 + EARLY * (BLOCK // 128):64]


def process_kernel(
    latent_h, gain, w_in_h, w_out_h, obs_src, obs_inst, upd, order, place,
    latent, w_in, w_out, wi, wo, normed, total, acc, load_sem, w_send, w_recv,
):
    x, z, c, y = coords()
    ys, zs, xs, others = lines()
    barrier = pltpu.get_barrier_semaphore()
    loads = [
        pltpu.make_async_copy(source, ref, load_sem.at[n])
        for n, (source, ref) in enumerate(((latent_h, latent), (w_in_h, w_in), (w_out_h, w_out)))
    ]
    for load in loads:
        load.start()
    signal(barrier, ys + xs + zs + others[:1])
    loads[0].wait()

    def prepare(i, _):
        at = pl.ds(pl.multiple_of(i * 256, 256), 256)
        normed[at] = normalise(latent[at], gain[...])
        total[at] = latent[at].astype(F32)
        return 0

    lax.fori_loop(0, ROWS // 256, prepare, 0)
    for load in loads[1:]:
        load.wait()
    pl.semaphore_wait(barrier, 10)

    def send(source, dest, phase, d, dev):
        pltpu.make_async_remote_copy(
            source, dest, w_send, w_recv.at[phase, d - 1], device_id=dev, device_id_type=MESH
        ).start()

    def wait(phase, d, n):
        part = wi.at[d - 1, pl.ds(0, 2 * n)]
        pltpu.make_async_copy(part, part, w_recv.at[phase, d - 1]).wait()

    def shard(first, second):
        def rows(i, _):
            at = pl.ds(pl.multiple_of(i * 512, 512), 512)
            inner = gelu(jnp.dot(normed[at], first, preferred_element_type=F32)).astype(BF16)
            total[at] += jnp.dot(inner, second, preferred_element_type=F32)
            return 0

        lax.fori_loop(0, ROWS // 512, rows, 0)

    pieces = (c * 8 + x, c * 8 + 4 + z)
    turns = (1, 3, 2)
    for d in turns:
        for piece in pieces:
            for own, ref in ((w_in, wi), (w_out, wo)):
                send(own.at[piece], ref.at[d - 1, piece], 0, d, ys[d - 1])
    shard(w_in[...].reshape(D, D), w_out[...].reshape(D, D))
    for d in turns:
        wait(0, d, 2)
        for n in range(3):
            for piece, line in zip(pieces, (xs, zs)):
                for ref in (wi, wo):
                    send(ref.at[d - 1, piece], ref.at[d - 1, piece], 1, d, line[n])
    sort(obs_src, obs_inst, order, place, acc)
    for d in turns:
        wait(1, d, 6)
        for ref in (wi, wo):
            half = ref.at[d - 1, pl.ds(c * 8, 8)]
            send(half, half, 2, d, others[0])
    for d in turns:
        wait(2, d, 8)
        shard(wi[d - 1].reshape(D, D), wo[d - 1].reshape(D, D))

    upd[...] = total[...].astype(BF16)
    for n in (2, 6, 8):
        for ref in (wi, wo):
            part = ref.at[pl.ds(0, 3), pl.ds(0, n)]
            pltpu.make_async_copy(part, part, w_send).wait()


def process(latent, gain, w_in, w_out, obs_src, obs_inst):
    vmem, any_ = pl.BlockSpec(memory_space=pltpu.VMEM), pl.BlockSpec(memory_space=pl.ANY)
    return pl.pallas_call(
        process_kernel,
        out_shape=(
            jax.ShapeDtypeStruct((ROWS, D), BF16),
            jax.ShapeDtypeStruct((96, 128), jnp.int32),
            jax.ShapeDtypeStruct((48, 128), jnp.int32),
        ),
        in_specs=[any_, vmem, any_, any_, vmem, vmem],
        out_specs=(vmem,) * 3,
        scratch_shapes=[
            pltpu.VMEM((ROWS, D), BF16),
            pltpu.VMEM((16, 32, D), BF16),
            pltpu.VMEM((16, 32, D), BF16),
            pltpu.VMEM((3, 16, 32, D), BF16),
            pltpu.VMEM((3, 16, 32, D), BF16),
            pltpu.VMEM((ROWS, D), BF16),
            pltpu.VMEM((ROWS, D), F32),
            pltpu.VMEM((160, 128), F32),
            pltpu.SemaphoreType.DMA((3,)),
            pltpu.SemaphoreType.DMA,
            pltpu.SemaphoreType.DMA((3, 3)),
        ],
        compiler_params=pltpu.CompilerParams(collective_id=0, has_side_effects=True, vmem_limit_bytes=56 << 20),
        name="process",
    )(
        latent, gain.reshape(1, D), w_in.reshape(16, 32, D), w_out.reshape(16, 32, D),
        obs_src.reshape(32, 128), obs_inst.reshape(32, 128),
    )


def exchange_kernel(
    upd_h, lists, order_h, order_vh, place_h, feat, embed, w_dec, w_feat, w_head, table, natural, late,
    upd, order_s, order, place_s,
    send, recv, tab, featb, feats, sfeats, picked, sides, wall, hidden, head, emb, dec, nat,
    load_sem, send_sem, recv_sem, out_sem, s2, s3,
):
    ys, zs, xs, others = lines()
    barrier = pltpu.get_barrier_semaphore()
    signal(barrier, ys + zs + xs + others)
    loads = [
        pltpu.make_async_copy(feat, featb, load_sem.at[0]),
        pltpu.make_async_copy(embed, emb, load_sem.at[1]),
        pltpu.make_async_copy(w_dec, wall.at[pl.ds(0, 512)], load_sem.at[2]),
        pltpu.make_async_copy(w_feat, wall.at[pl.ds(512, 128)], load_sem.at[3]),
        pltpu.make_async_copy(w_head, head, load_sem.at[4]),
        pltpu.make_async_copy(order_h, order_s, load_sem.at[5]),
        pltpu.make_async_copy(order_vh, order, load_sem.at[6]),
        pltpu.make_async_copy(place_h, place_s, load_sem.at[7]),
    ]
    rows_in = pltpu.make_async_copy(upd_h, upd, load_sem.at[8])
    rows_in.start()
    for load in loads:
        load.start()

    lane = lax.broadcasted_iota(jnp.int32, (CAP, NDEV), 1)
    cell = lax.broadcasted_iota(jnp.int32, (CAP, ROWS), 1)

    def gather(j, source):
        def hot(i):
            pp, tt = partner(j * PER + i)
            column = jnp.sum(jnp.where(lane == pp * 4 + tt, lists[...], 0).astype(F32), axis=1, keepdims=True)
            return jnp.where(cell == column.astype(jnp.int32), 1.0, 0.0).astype(BF16)

        chosen = jnp.concatenate([hot(i) for i in range(PER)], axis=0)
        rows = jnp.dot(chosen, source[...], preferred_element_type=F32).astype(BF16)
        send[pl.ds(j * PER, PER)] = rows.reshape(PER, CAP, D)

    def put(k):
        pltpu.make_async_remote_copy(
            send.at[k], recv.at[k], send_sem, recv_sem.at[k // PER], device_id=partner(k), device_id_type=MESH
        ).start()

    def start(lo, hi):
        def one(k, _):
            put(k)
            return 0

        lax.fori_loop(lo, hi, one, 0)

    def chunks(lo, hi, source):
        def one(j, _):
            gather(j, source)
            start(j * PER, j * PER + PER)
            return 0

        lax.fori_loop(lo, hi, one, 0)

    rows_in.wait()
    gather(0, upd)
    recv[0] = send[0]
    pl.semaphore_wait(barrier, 13)
    signal(s2, zs)
    gather(1, upd)
    pl.semaphore_wait(s2, 3)
    signal(s3, xs + others)
    gather(2, upd)
    pl.semaphore_wait(s3, 7)
    start(1, 3 * PER)
    chunks(3, CHUNKS, upd)
    for load in loads:
        load.wait()
    load_decoder(emb, wall)
    feats[...] = featb[...].astype(F32)
    pick_sides(order_s, order, feats, sfeats, sides)

    def spread_own(i, _):
        widen(tab, i * CROWS, upd[pl.ds(pl.multiple_of(i * CROWS, CROWS), CROWS)])
        return 0

    lax.fori_loop(0, ROWS // CROWS, spread_own, 0)

    rest = pltpu.make_async_copy(recv, table, out_sem.at[0])
    nat_out = pltpu.make_async_copy(nat, natural, out_sem.at[1])

    def step(s, _):
        j = s - 1

        @pl.when(j == 0)
        def _():
            pltpu.make_async_copy(recv.at[pl.ds(1, PER - 1)], recv.at[pl.ds(1, PER - 1)], recv_sem.at[0]).wait()

        @pl.when(jnp.logical_and(j > 0, j < CHUNKS))
        def _():
            part = recv.at[pl.ds(j * PER, PER)]
            pltpu.make_async_copy(part, part, recv_sem.at[j]).wait()

        @pl.when(jnp.logical_and(j >= 0, j < CHUNKS))
        def _():
            widen(tab, ROWS + j * CROWS, recv[pl.ds(j * PER, PER)].reshape(CROWS, D))

        @pl.when(s == EVENTS)
        def _():
            rest.start()

        b = (2 * s + 1) // 5 + s // 14 - s // 15

        @pl.when(step_of(b) == s)
        def _():
            at = pl.ds(pl.multiple_of(b * BLOCK, BLOCK), BLOCK)
            dec[at] = decode_block(b, order_s, tab, picked, sides, wall, hidden, head)

        @pl.when(s == step_of(EARLY - 1) + 1)
        def _():
            def back(n, _):
                for u in range(64):
                    j = n * 64 + u
                    nat[pl.ds(j, 1), :] = dec[pl.ds(place_s[j], 1), :]
                return 0

            lax.fori_loop(0, OBS // 64, back, 0)
            nat_out.start()

        return 0

    lax.fori_loop(0, EVENTS + 1, step, 0)
    last = pltpu.make_async_copy(dec.at[pl.ds(EARLY * BLOCK, LATE)], late, out_sem.at[2])
    last.start()
    rest.wait()
    nat_out.wait()
    last.wait()
    pltpu.make_async_copy(send.at[pl.ds(0, NDEV - 1)], send.at[pl.ds(0, NDEV - 1)], send_sem).wait()


def exchange(upd, send_rows, order, place, feat, embed, w_dec, w_feat, w_head):
    vmem, any_ = pl.BlockSpec(memory_space=pltpu.VMEM), pl.BlockSpec(memory_space=pl.ANY)
    return pl.pallas_call(
        exchange_kernel,
        out_shape=(
            jax.ShapeDtypeStruct((NDEV, CAP, D), BF16),
            jax.ShapeDtypeStruct((OBS, 128), F32),
            jax.ShapeDtypeStruct((LATE, 128), F32),
        ),
        in_specs=[any_, vmem] + [any_] * 8,
        out_specs=(any_, any_, any_),
        scratch_shapes=[
            pltpu.VMEM((ROWS, D), BF16),
            pltpu.SMEM((96 * 128,), jnp.int32),
            pltpu.VMEM((96, 128), jnp.int32),
            pltpu.SMEM((48 * 128,), jnp.int32),
            pltpu.VMEM((NDEV, CAP, D), BF16),
            pltpu.VMEM((NDEV, CAP, D), BF16),
            pltpu.VMEM((4 * TABLE + 8, 128), F32),
            pltpu.VMEM((OBS, 128), BF16),
            pltpu.VMEM((OBS, 128), F32),
            pltpu.VMEM((OBS, 128), F32),
            pltpu.VMEM((4 * BLOCK + 8, 128), F32),
            pltpu.VMEM((OBS, SIDE), BF16),
            pltpu.VMEM((512 + SIDE, FF), BF16),
            pltpu.VMEM((BLOCK, FF), BF16),
            pltpu.VMEM((FF, 128), BF16),
            pltpu.VMEM((32, FF), F32),
            pltpu.VMEM((OBS, 128), F32),
            pltpu.VMEM((OBS, 128), F32),
            pltpu.SemaphoreType.DMA((9,)),
            pltpu.SemaphoreType.DMA,
            pltpu.SemaphoreType.DMA((CHUNKS,)),
            pltpu.SemaphoreType.DMA((3,)),
            pltpu.SemaphoreType.REGULAR,
            pltpu.SemaphoreType.REGULAR,
        ],
        compiler_params=pltpu.CompilerParams(collective_id=1, has_side_effects=True, vmem_limit_bytes=60 << 20),
        name="exchange",
    )(upd, send_rows.T, order.reshape(-1), order, place.reshape(-1), feat, embed, w_dec, w_feat, w_head)


def finish_kernel(
    place, order, order_h, upd, natural, late, table, feat, embed, w_dec, w_feat, w_head, latent_out, decoded,
    buf, tail, lat, tabb, tab, featb, feats, sfeats, picked, sides, wall, hidden, head, emb, order_s, order_v, sem, load_sem,
):
    ins = [
        pltpu.make_async_copy(natural, buf, sem.at[1]),
        pltpu.make_async_copy(late, tail, sem.at[2]),
        pltpu.make_async_copy(upd, lat, sem.at[0]),
    ]
    for copy in ins:
        copy.start()
    for copy in ins:
        copy.wait()
    keep = pltpu.make_async_copy(lat, latent_out, sem.at[3])
    keep.start()

    def scatter(numbers, start, n):
        def move(i, _):
            for u in range(64):
                j = i * 64 + u
                buf[pl.ds(numbers[start + j], 1), :] = tail[pl.ds(j, 1), :]
            return 0

        lax.fori_loop(0, n // 64, move, 0)

    scatter(place, 40 * 128, LATE)

    def missed(b):
        last = place[(32 + b) * 128 + 127]
        return jnp.where(last < ROWS, 0, 1 + (last - ROWS) // CROWS) > step_of(b)

    any_missed = missed(0)
    for b in range(1, BLOCKS):
        any_missed = jnp.logical_or(any_missed, missed(b))

    @pl.when(any_missed)
    def _():
        loads = [
            pltpu.make_async_copy(feat, featb, load_sem.at[0]),
            pltpu.make_async_copy(embed, emb, load_sem.at[1]),
            pltpu.make_async_copy(w_dec, wall.at[pl.ds(0, 512)], load_sem.at[2]),
            pltpu.make_async_copy(w_feat, wall.at[pl.ds(512, 128)], load_sem.at[3]),
            pltpu.make_async_copy(w_head, head, load_sem.at[4]),
            pltpu.make_async_copy(table, tabb, load_sem.at[5]),
            pltpu.make_async_copy(order, order_v, load_sem.at[6]),
            pltpu.make_async_copy(order_h, order_s, load_sem.at[7]),
        ]
        for load in loads:
            load.start()
        for load in loads:
            load.wait()
        load_decoder(emb, wall)
        feats[...] = featb[...].astype(F32)
        pick_sides(order_s, order_v, feats, sfeats, sides)

        def spread_own(n, _):
            widen(tab, n * CROWS, lat[pl.ds(pl.multiple_of(n * CROWS, CROWS), CROWS)])
            return 0

        lax.fori_loop(0, ROWS // CROWS, spread_own, 0)

        def spread(n, _):
            widen(tab, ROWS + n * CROWS, tabb[pl.ds(n * PER, PER)].reshape(CROWS, D))
            return 0

        lax.fori_loop(0, CHUNKS, spread, 0)

        def again(b, _):
            @pl.when(missed(b))
            def _():
                tail[0:BLOCK] = decode_block(b, order_s, tab, picked, sides, wall, hidden, head)
                scatter(order_s, OBS + b * BLOCK, BLOCK)

            return 0

        lax.fori_loop(0, BLOCKS, again, 0)

    done = pltpu.make_async_copy(buf, decoded, sem.at[4])
    done.start()
    done.wait()
    keep.wait()


def finish(place, order, upd, natural, late, table, feat, embed, w_dec, w_feat, w_head):
    any_ = pl.BlockSpec(memory_space=pl.ANY)
    return pl.pallas_call(
        finish_kernel,
        out_shape=(jax.ShapeDtypeStruct((ROWS, D), BF16), jax.ShapeDtypeStruct((OBS, 128), F32)),
        grid_spec=pltpu.PrefetchScalarGridSpec(
            num_scalar_prefetch=1,
            grid=(1,),
            in_specs=[any_] * 11,
            out_specs=(any_, any_),
            scratch_shapes=[
                pltpu.VMEM((OBS, 128), F32),
                pltpu.VMEM((LATE, 128), F32),
                pltpu.VMEM((ROWS, D), BF16),
                pltpu.VMEM((NDEV, CAP, D), BF16),
                pltpu.VMEM((4 * TABLE + 8, 128), F32),
                pltpu.VMEM((OBS, 128), BF16),
                pltpu.VMEM((OBS, 128), F32),
                pltpu.VMEM((OBS, 128), F32),
                pltpu.VMEM((4 * BLOCK + 8, 128), F32),
                pltpu.VMEM((OBS, SIDE), BF16),
                pltpu.VMEM((512 + SIDE, FF), BF16),
                pltpu.VMEM((BLOCK, FF), BF16),
                pltpu.VMEM((FF, 128), BF16),
                pltpu.VMEM((32, FF), F32),
                pltpu.SMEM((96 * 128,), jnp.int32),
                pltpu.VMEM((96, 128), jnp.int32),
                pltpu.SemaphoreType.DMA((5,)),
                pltpu.SemaphoreType.DMA((8,)),
            ],
        ),
        compiler_params=pltpu.CompilerParams(vmem_limit_bytes=56 << 20, dimension_semantics=("arbitrary",)),
        name="finish",
    )(place.reshape(-1), order, order.reshape(-1), upd, natural, late, table, feat, embed, w_dec, w_feat, w_head)


def local(latent, norm_gain, w_in, w_out, send_rows, obs_src, obs_feat, obs_inst, inst_embed, w_dec, w_feat, w_head):
    upd, order, place = process(latent, norm_gain, w_in, w_out, obs_src, obs_inst)
    table, natural, late = exchange(upd, send_rows, order, place, obs_feat, inst_embed, w_dec, w_feat, w_head)
    return finish(place, order, upd, natural, late, table, obs_feat, inst_embed, w_dec, w_feat, w_head)


def solution(mesh):
    in_specs = (
        P(("pix", "tp"), None),
        P(),
        P(None, "tp"),
        P("tp", None),
        P(("pix", "tp"), None),
        P(("pix", "tp")),
        P(("pix", "tp"), None),
        P(("pix", "tp")),
        P(),
        P(),
        P(),
        P(),
    )
    out_specs = (P(("pix", "tp"), None), P(("pix", "tp"), None))
    return jax.shard_map(local, mesh=mesh, in_specs=in_specs, out_specs=out_specs, check_vma=False)
```
